32 devices in a mesh: diag: 4 (over z), long: 8 (over y, x, core).
Axes of the slice: x: 2, y: 2, z: 4, core: 2. Of those that a mesh axis runs over, the one named last changes fastest.
Arguments:
- tiles: bfloat16 [4, 8, 512, 128, 128], P('diag', 'long'), may hold values from -0.0546875 to 0.0546875
- tile_rows: int32 [4, 8, 512], P('diag', 'long'), may hold values from 0 to 23, as said below
- tile_cols: int32 [4, 8, 512], P('diag', 'long'), may hold values from 0 to 47, as said below
- tile_counts: int32 [4, 8], P('diag', 'long'), may hold values from 0 to 512, as said below
- block_x: bfloat16 [16, 24576], P(None, 'long'), may hold values from -16 to 16
- block_p: bfloat16 [16, 24576], P(None, 'long'), may hold values from -16 to 16
Outputs:
- ritz_basis: float32 [48, 24576], P(None, 'long')
- ritz_image: float32 [48, 24576], P(None, 'long')
- ritz_matrix: float32 [48, 48], replicated
The draws below stay inside these ranges and needn't reach their ends.
Inputs may be any that keep to these rules, and one draw needn't show every extreme that they name: `tile_rows`: each entry is a tile row of the row panel of its grid position. `tile_cols`: each entry is a tile column of the two panels of the segment of its grid position; for live entries the global tile column never exceeds the global tile row, and no pair of tile row and column repeats within one list. `tile_counts`: entries of a list past its count are ignored. A count never exceeds the pairs of its grid position on or below the diagonal; the last grid column of grid row 0 is full.
All inputs are finite; a program needn't handle non-finite values.
Results may differ from the reference program's by a relative error of at most 0.0004.
The reference program's roundings to bfloat16 on the way (of `search`) count: a program that leaves them out, or rounds other values in their place, can miss the bound.
Values may be sent and summed in bfloat16 or wider, within the bound.
A program may use at most 128 MiB of HBM per device.

```python
import jax
import jax.numpy as jnp
from jax import lax

TILE = 128
BLOCK = 16
PT = 24
TILES = 512
SUBSPACE = 48
NTOT = 24576
N_DIAG = 4
N_LONG = 8


def tile_layout(key):
    pairs = 2 * PT * PT
    index_all = jnp.arange(pairs, dtype=jnp.int32)
    row_of = index_all // (2 * PT)
    col_of = index_all % (2 * PT)
    diag_ids = jnp.arange(N_DIAG, dtype=jnp.int32)[:, None]
    long_ids = jnp.arange(N_LONG, dtype=jnp.int32)[None, :]
    folded = long_ids < 2 * diag_ids
    row_panel = jnp.where(folded, N_LONG - 1 - long_ids, long_ids)[:, :, None]
    segment_id = jnp.where(folded, N_DIAG - 1 - diag_ids, diag_ids)[:, :, None]
    allowed = 2 * segment_id * PT + col_of[None, None, :] <= row_panel * PT + row_of[None, None, :]
    scores = jax.random.randint(key, (N_DIAG, N_LONG, pairs), 0, 1 << 14) * pairs + index_all[None, None, :]
    scores = jnp.where(allowed, scores, -1 - index_all[None, None, :])
    _, chosen = jax.lax.top_k(scores, TILES)
    rows = row_of[chosen]
    cols = col_of[chosen]
    avail = jnp.sum(allowed.astype(jnp.int32), axis=2)
    cutoff = jax.random.randint(jax.random.fold_in(key, 1), (N_DIAG, N_LONG), 0, TILES // 2 + 1)
    counts = jnp.minimum(avail, TILES - cutoff)
    counts = counts.at[0, N_LONG - 1].set(jnp.minimum(avail[0, N_LONG - 1], TILES))
    return (rows.astype(jnp.int32), cols.astype(jnp.int32), counts.astype(jnp.int32))


def draw_tile_rows(key, part):
    layout = tile_layout(key)
    return layout[0]


def draw_tile_cols(key, part):
    layout = tile_layout(key)
    return layout[1]


def draw_tile_counts(key, part):
    layout = tile_layout(key)
    return layout[2]


def scaled_rows(base, rise):
    ramp = 1.0 + rise * jnp.arange(NTOT, dtype=jnp.float32) / NTOT
    return (base * ramp[None, :]).astype(jnp.bfloat16)


def draw_block_x(key, part):
    key = jax.random.fold_in(key, 11)
    base = jnp.clip(jax.random.normal(key, (BLOCK, NTOT), jnp.float32), -4.0, 4.0)
    rise = 2.0
    return scaled_rows(base, rise)


def draw_block_p(key, part):
    key = jax.random.fold_in(key, 23)
    base = jnp.clip(jax.random.normal(key, (BLOCK, NTOT), jnp.float32), -4.0, 4.0)
    rise = 2.0
    return scaled_rows(base, rise)


def shard_levels(own_key, dims, pieces, least, top_value):
    loudness, own = 1.0, jax.random.fold_in(own_key, 6)
    for axis_at, shards_of in pieces:
        draws = jnp.exp(jax.random.uniform(jax.random.fold_in(own, axis_at), (shards_of,), jnp.float32, least / len(pieces), top_value / len(pieces)))
        loudness = loudness * jnp.repeat(draws, dims[axis_at] // shards_of).reshape([-1 if axis == axis_at else 1 for axis in range(len(dims))])
    return loudness


def normal_values(key, shape, spread, bound, split=(), kind=jnp.bfloat16):
    factor_of = shard_levels(key, shape, split, -0.22, 0.18) if split else 1.0
    entries = jax.random.normal(key, shape, jnp.float32) * spread * factor_of
    return jnp.minimum(jnp.maximum(entries, -bound), bound).astype(kind)


def setup_inputs(seed: int = 0) -> dict:
    seeds = jax.random.split(jax.random.key(seed), 7)
    tiles = normal_values(seeds[0], (N_DIAG, N_LONG, TILES, TILE, TILE), (TILE * N_DIAG * TILES // PT) ** -0.5, 0.0546875, ((0, 4), (1, 8)))
    tile_rows = draw_tile_rows(jax.random.fold_in(seeds[6], 71), 0)
    tile_cols = draw_tile_cols(jax.random.fold_in(seeds[6], 71), 0)
    tile_counts = draw_tile_counts(jax.random.fold_in(seeds[6], 71), 0)
    block_x = draw_block_x(jax.random.fold_in(seeds[6], 71), 0)
    block_p = draw_block_p(jax.random.fold_in(seeds[6], 71), 0)
    return {"tiles": tiles, "tile_rows": tile_rows, "tile_cols": tile_cols, "tile_counts": tile_counts, "block_x": block_x, "block_p": block_p}


def apply_hamiltonian(vectors, tiles, tile_rows, tile_cols, tile_counts):
    count_vec = vectors.shape[0]
    tiled = vectors.reshape(count_vec, NTOT // TILE, TILE).astype(jnp.float32)
    diag_ids = jnp.repeat(jnp.arange(N_DIAG, dtype=jnp.int32), N_LONG)
    long_ids = jnp.tile(jnp.arange(N_LONG, dtype=jnp.int32), N_DIAG)
    slots = jnp.arange(TILES, dtype=jnp.int32)

    def one_device(accum, items):
        tile_block, rows, cols, count, diag_id, long_id = items
        folded = long_id < 2 * diag_id
        row_panel = jnp.where(folded, N_LONG - 1 - long_id, long_id).astype(jnp.int32)
        segment_id = jnp.where(folded, N_DIAG - 1 - diag_id, diag_id).astype(jnp.int32)
        rows_glob = (row_panel * PT + rows).astype(jnp.int32)
        cols_glob = (2 * segment_id * PT + cols).astype(jnp.int32)
        valid = (slots < count).astype(jnp.float32)
        weight = jnp.where(rows_glob == cols_glob, 0.5, 1.0).astype(jnp.float32) * valid
        tile_float = tile_block.astype(jnp.float32)
        forward = jnp.einsum('kab,vkb->vka', tile_float, tiled[:, cols_glob, :])
        accum = accum.at[:, rows_glob, :].add(forward * weight[None, :, None])
        backward = jnp.einsum('kab,vka->vkb', tile_float, tiled[:, rows_glob, :])
        accum = accum.at[:, cols_glob, :].add(backward * weight[None, :, None])
        return (accum, None)
    start = jnp.zeros((count_vec, NTOT // TILE, TILE), jnp.float32)
    items = (tiles.reshape(-1, TILES, TILE, TILE), tile_rows.reshape(-1, TILES), tile_cols.reshape(-1, TILES), tile_counts.reshape(-1), diag_ids, long_ids)
    accum, _ = lax.scan(one_device, start, items)
    return accum.reshape(count_vec, NTOT)

def reference(tiles, tile_rows, tile_cols, tile_counts, block_x, block_p):
    highest = lax.Precision.HIGHEST
    first = apply_hamiltonian(jnp.concatenate([block_x, block_p], 0), tiles, tile_rows, tile_cols, tile_counts)
    image_x = first[:BLOCK]
    image_p = first[BLOCK:]
    block_float = block_x.astype(jnp.float32)
    numerator = jnp.sum(block_float * image_x, axis=1)
    denominator = jnp.sum(block_float * block_float, axis=1)
    quotient = numerator / denominator
    search = (image_x - quotient[:, None] * block_float).astype(jnp.bfloat16)
    image_w = apply_hamiltonian(search, tiles, tile_rows, tile_cols, tile_counts)
    basis_in = jnp.concatenate([block_x, search, block_p], 0).astype(jnp.float32)
    himage = jnp.concatenate([image_x, image_w, image_p], 0)
    gram = jnp.dot(basis_in, basis_in.T, precision=highest)
    projected = jnp.dot(basis_in, himage.T, precision=highest)
    factor = jnp.linalg.cholesky(gram)
    inverse = jax.scipy.linalg.solve_triangular(factor, jnp.eye(SUBSPACE, dtype=jnp.float32), lower=True)
    ritz_basis = jnp.dot(inverse, basis_in, precision=highest)
    ritz_image = jnp.dot(inverse, himage, precision=highest)
    reduced = jnp.dot(jnp.dot(inverse, projected, precision=highest), inverse.T, precision=highest)
    ritz_matrix = 0.5 * (reduced + reduced.T)
    return (ritz_basis, ritz_image, ritz_matrix)
```

```python
import functools

import jax
import jax.numpy as jnp
from jax import lax
from jax.experimental import pallas as pl
from jax.experimental.pallas import tpu as pltpu
from jax.sharding import PartitionSpec as P

HIGHEST = lax.Precision.HIGHEST
STEP = 64
UNROLL = 8


def tile_kernel(rows_ref, cols_ref, meta_ref, vec_ref, tile_ref, out_ref):
    edge = tile_ref.shape[-1]
    base = pl.program_id(0) * STEP

    @pl.when(pl.program_id(0) == 0)
    def _():
        out_ref[...] = jnp.zeros_like(out_ref)

    count, row_off, col_off = meta_ref[0], meta_ref[1], meta_ref[2]
    live = jnp.clip(count - base, 0, STEP)

    def group(i, carry):
        spots = []
        for u in range(UNROLL):
            k = i * UNROLL + u
            row = rows_ref[base + k] + row_off
            col = cols_ref[base + k] + col_off
            weight = jnp.where(row == col, 0.5, 1.0).astype(jnp.float32)
            weight = jnp.where(base + k < count, weight, 0.0)
            row_at = pl.ds(pl.multiple_of(row * edge, edge), edge)
            col_at = pl.ds(pl.multiple_of(col * edge, edge), edge)
            tile = tile_ref[k]
            forward = lax.dot_general(
                vec_ref[:, col_at],
                tile,
                (((1,), (1,)), ((), ())),
                preferred_element_type=jnp.float32,
            )
            backward = jnp.dot(vec_ref[:, row_at], tile, preferred_element_type=jnp.float32)
            spots.append((row_at, col_at, forward * weight, backward * weight))
        for row_at, col_at, forward, backward in spots:
            out_ref[:, row_at] += forward
            out_ref[:, col_at] += backward
        return carry

    lax.fori_loop(0, (live + UNROLL - 1) // UNROLL, group, 0)


def apply_tiles(tiles, rows, cols, meta, vectors):
    slots, edge = tiles.shape[0], tiles.shape[-1]
    width, states = vectors.shape
    smem = pl.BlockSpec(memory_space=pltpu.SMEM)
    return pl.pallas_call(
        tile_kernel,
        grid=(slots // STEP,),
        in_specs=[
            smem,
            smem,
            smem,
            pl.BlockSpec(memory_space=pltpu.VMEM),
            pl.BlockSpec((STEP, edge, edge), lambda i: (i, 0, 0)),
        ],
        out_specs=pl.BlockSpec((width, states), lambda i: (0, 0)),
        out_shape=jax.ShapeDtypeStruct((width, states), jnp.float32),
        compiler_params=pltpu.CompilerParams(vmem_limit_bytes=40 << 20),
        cost_estimate=pl.CostEstimate(
            flops=4 * slots * edge * edge * width,
            bytes_accessed=2 * slots * edge * edge,
            transcendentals=0,
        ),
    )(rows, cols, meta, vectors, tiles)


def ritz_kernel(gram_ref, proj_ref, basis_ref, image_ref, rb_ref, ri_ref, rm_ref):
    size = gram_ref.shape[0]
    lane = lax.broadcasted_iota(jnp.int32, (size, size), 1)
    row = lax.broadcasted_iota(jnp.int32, (size, size), 0)
    below = lax.broadcasted_iota(jnp.int32, (size, 1), 0)
    left = gram_ref[...]
    right = jnp.where(lane == row, 1.0, 0.0).astype(jnp.float32)
    pivots = jnp.zeros((size, 1), jnp.float32)
    for k in range(size):
        pivot = left[k : k + 1, k : k + 1]
        pivots = jnp.where(below == k, pivot, pivots)
        scale = jnp.where(below > k, left[:, k : k + 1] * (1.0 / pivot), 0.0)
        left_row, right_row = left[k : k + 1, :], right[k : k + 1, :]
        left = left - scale * left_row
        right = right - scale * right_row
    inverse = right * (1.0 / jnp.sqrt(pivots))
    nt = (((1,), (1,)), ((), ()))
    half = jnp.dot(inverse, proj_ref[...], precision=HIGHEST, preferred_element_type=jnp.float32)
    one = lax.dot_general(half, inverse, nt, precision=HIGHEST, preferred_element_type=jnp.float32)
    two = lax.dot_general(inverse, half, nt, precision=HIGHEST, preferred_element_type=jnp.float32)
    rm_ref[...] = 0.5 * (one + two)
    rb_ref[...] = jnp.dot(
        inverse, basis_ref[...].astype(jnp.float32), precision=HIGHEST, preferred_element_type=jnp.float32
    )
    ri_ref[...] = jnp.dot(
        inverse, image_ref[...], precision=HIGHEST, preferred_element_type=jnp.float32
    )


def ritz(gram, projected, basis, image):
    vmem = pl.BlockSpec(memory_space=pltpu.VMEM)
    like = jax.ShapeDtypeStruct(image.shape, jnp.float32)
    return pl.pallas_call(
        ritz_kernel,
        in_specs=[vmem] * 4,
        out_specs=[vmem] * 3,
        out_shape=[like, like, jax.ShapeDtypeStruct(gram.shape, jnp.float32)],
        compiler_params=pltpu.CompilerParams(vmem_limit_bytes=40 << 20),
    )(gram, projected, basis, image)


def local(tiles, tile_rows, tile_cols, tile_counts, block_x, block_p):
    tile_block = tiles[0, 0]
    rows = tile_rows[0, 0]
    cols = tile_cols[0, 0]
    edge = tile_block.shape[-1]
    panel_tiles = block_x.shape[1] // edge
    diag_index = lax.axis_index("diag")
    long_index = lax.axis_index("long")
    long_size = lax.axis_size("long")
    diag_size = lax.axis_size("diag")
    folded = long_index < 2 * diag_index
    row_panel = jnp.where(folded, long_size - 1 - long_index, long_index)
    segment_id = jnp.where(folded, diag_size - 1 - diag_index, diag_index)
    meta = jnp.stack(
        [tile_counts[0, 0], row_panel * panel_tiles, 2 * segment_id * panel_tiles]
    ).astype(jnp.int32)

    def apply_hamiltonian(vectors):
        whole = lax.all_gather(vectors, "long", axis=1, tiled=True)
        spread = apply_tiles(tile_block, rows, cols, meta, whole)
        total = lax.psum_scatter(spread, "long", scatter_dimension=1, tiled=True)
        return lax.psum(total, "diag")

    width = block_x.shape[0]
    first = apply_hamiltonian(jnp.concatenate([block_x, block_p], 0))
    image_x = first[:width]
    image_p = first[width:]
    block_float = block_x.astype(jnp.float32)
    numerator, denominator = lax.psum(
        (jnp.sum(block_float * image_x, axis=1), jnp.sum(block_float * block_float, axis=1)), "long"
    )
    quotient = numerator / denominator
    search = (image_x - quotient[:, None] * block_float).astype(jnp.bfloat16)
    image_w = apply_hamiltonian(search)
    basis_in = jnp.concatenate([block_x, search, block_p], 0)
    himage = jnp.concatenate([image_x, image_w, image_p], 0)
    basis_float = basis_in.astype(jnp.float32)
    gram, projected = lax.psum(
        (
            jnp.dot(basis_float, basis_float.T, precision=HIGHEST),
            jnp.dot(basis_float, himage.T, precision=HIGHEST),
        ),
        "long",
    )
    return tuple(ritz(gram, projected, basis_in, himage))


def solution(mesh):
    return jax.shard_map(
        local,
        mesh=mesh,
        in_specs=(
            P("diag", "long", None, None, None),
            P("diag", "long", None),
            P("diag", "long", None),
            P("diag", "long"),
            P(None, "long"),
            P(None, "long"),
        ),
        out_specs=(P(None, "long"), P(None, "long"), P()),
        check_vma=False,
    )
```

```python
import functools

import jax
import jax.numpy as jnp
from jax import lax
from jax.experimental import pallas as pl
from jax.experimental.pallas import tpu as pltpu
from jax.sharding import PartitionSpec as P

HIGHEST = lax.Precision.HIGHEST
STEP = 64
UNROLL = 8


def tile_kernel(rows_ref, cols_ref, meta_ref, vec_ref, tile_ref, out_ref):
    edge = tile_ref.shape[-1]
    row_lane = out_ref.shape[1] // 3 * 2
    base = pl.program_id(0) * STEP

    @pl.when(pl.program_id(0) == 0)
    def _():
        out_ref[...] = jnp.zeros_like(out_ref)

    count, row_off, col_off = meta_ref[0], meta_ref[1], meta_ref[2]
    live = jnp.clip(count - base, 0, STEP)

    def group(i, carry):
        spots = []
        for u in range(UNROLL):
            k = i * UNROLL + u
            row = rows_ref[base + k]
            col = cols_ref[base + k]
            weight = jnp.where(row + row_off == col + col_off, 0.5, 1.0).astype(jnp.float32)
            weight = jnp.where(base + k < count, weight, 0.0)
            row_at = pl.ds(pl.multiple_of(row * edge + row_lane, edge), edge)
            col_at = pl.ds(pl.multiple_of(col * edge, edge), edge)
            tile = tile_ref[k]
            forward = lax.dot_general(
                vec_ref[:, col_at],
                tile,
                (((1,), (1,)), ((), ())),
                preferred_element_type=jnp.float32,
            )
            backward = jnp.dot(vec_ref[:, row_at], tile, preferred_element_type=jnp.float32)
            spots.append((row_at, col_at, forward * weight, backward * weight))
        for row_at, col_at, forward, backward in spots:
            out_ref[:, row_at] += forward
            out_ref[:, col_at] += backward
        return carry

    lax.fori_loop(0, (live + UNROLL - 1) // UNROLL, group, 0)


def apply_tiles(tiles, rows, cols, meta, vectors):
    slots, edge = tiles.shape[0], tiles.shape[-1]
    width, states = vectors.shape
    smem = pl.BlockSpec(memory_space=pltpu.SMEM)
    return pl.pallas_call(
        tile_kernel,
        grid=(slots // STEP,),
        in_specs=[
            smem,
            smem,
            smem,
            pl.BlockSpec(memory_space=pltpu.VMEM),
            pl.BlockSpec((STEP, edge, edge), lambda i: (i, 0, 0)),
        ],
        out_specs=pl.BlockSpec((width, states), lambda i: (0, 0)),
        out_shape=jax.ShapeDtypeStruct((width, states), jnp.float32),
        compiler_params=pltpu.CompilerParams(vmem_limit_bytes=40 << 20),
        cost_estimate=pl.CostEstimate(
            flops=4 * slots * edge * edge * width,
            bytes_accessed=2 * slots * edge * edge,
            transcendentals=0,
        ),
    )(rows, cols, meta, vectors, tiles)


def ritz_kernel(sums_ref, basis_ref, image_ref, rb_ref, ri_ref, rm_ref):
    size = sums_ref.shape[0]
    lane = lax.broadcasted_iota(jnp.int32, (size, size), 1)
    row = lax.broadcasted_iota(jnp.int32, (size, size), 0)
    below = lax.broadcasted_iota(jnp.int32, (size, 1), 0)
    sums = sums_ref[...]
    left = sums[:, :size]
    right = jnp.where(lane == row, 1.0, 0.0).astype(jnp.float32)
    pivots = jnp.zeros((size, 1), jnp.float32)
    for k in range(size):
        pivot = left[k : k + 1, k : k + 1]
        pivots = jnp.where(below == k, pivot, pivots)
        scale = jnp.where(below > k, left[:, k : k + 1] * (1.0 / pivot), 0.0)
        left_row, right_row = left[k : k + 1, :], right[k : k + 1, :]
        left = left - scale * left_row
        right = right - scale * right_row
    inverse = right * (1.0 / jnp.sqrt(pivots))
    nt = (((1,), (1,)), ((), ()))
    half = jnp.dot(inverse, sums[:, size : 2 * size], precision=HIGHEST, preferred_element_type=jnp.float32)
    one = lax.dot_general(half, inverse, nt, precision=HIGHEST, preferred_element_type=jnp.float32)
    two = lax.dot_general(inverse, half, nt, precision=HIGHEST, preferred_element_type=jnp.float32)
    rm_ref[...] = 0.5 * (one + two)
    rb_ref[...] = jnp.dot(
        inverse, basis_ref[...].astype(jnp.float32), precision=HIGHEST, preferred_element_type=jnp.float32
    )
    ri_ref[...] = jnp.dot(
        inverse, image_ref[...], precision=HIGHEST, preferred_element_type=jnp.float32
    )


def ritz(sums, basis, image):
    vmem = pl.BlockSpec(memory_space=pltpu.VMEM)
    like = jax.ShapeDtypeStruct(image.shape, jnp.float32)
    return pl.pallas_call(
        ritz_kernel,
        in_specs=[vmem] * 3,
        out_specs=[vmem] * 3,
        out_shape=[like, like, jax.ShapeDtypeStruct((sums.shape[0], sums.shape[0]), jnp.float32)],
        compiler_params=pltpu.CompilerParams(vmem_limit_bytes=40 << 20),
    )(sums, basis, image)


class Place:
    def __init__(self, diag_size, long_size):
        self.diag_size, self.long_size = diag_size, long_size
        self.chips = long_size // 2
        self.d = lax.axis_index("diag")
        self.c = lax.axis_index("long")
        self.q, self.k = self.c // 2, self.c % 2
        self.partner = self.q * 2 + 1 - self.k
        self.mirror = long_size - 1 - self.c
        self.folded = self.q < self.d
        self.segment = self.segment_of(self.q)
        self.mirror_folded = self.mirror // 2 < self.d

    def segment_of(self, chip):
        return jnp.where(chip < self.d, self.diag_size - 1 - self.d, self.d)

    def copy(self, src, dst, send, recv, d, c):
        return pltpu.make_async_remote_copy(
            src_ref=src,
            dst_ref=dst,
            send_sem=send,
            recv_sem=recv,
            device_id=(d, c),
            device_id_type=pl.DeviceIdType.MESH,
        )

    def enter(self):
        barrier = pltpu.get_barrier_semaphore()
        peers = [(self.d, (self.c + o) % self.long_size) for o in range(1, self.long_size)]
        peers += [((self.d + o) % self.diag_size, self.c) for o in range(1, self.diag_size)]
        for peer in peers:
            pl.semaphore_signal(barrier, inc=1, device_id=peer, device_id_type=pl.DeviceIdType.MESH)
        pl.semaphore_wait(barrier, len(peers))


def spread_panels(at, own, vec, send, recv):
    def to_chip(t):
        return at.copy(own, vec.at[at.k], send.at[t], recv.at[0], at.d, 2 * t + at.k)

    def wanted(t):
        return jnp.logical_and(at.q != t, at.segment_of(t) == at.q)

    mirror = at.copy(own, vec.at[2], send.at[at.chips], recv.at[1], at.d, at.mirror)
    for t in range(at.chips):
        @pl.when(wanted(t))
        def _():
            to_chip(t).start()

    @pl.when(at.mirror_folded)
    def _():
        mirror.start()

    pair = at.copy(
        vec.at[at.k], vec.at[at.k], send.at[at.chips + 1], recv.at[2], at.d, at.partner
    )

    @pl.when(at.segment == at.q)
    def _():
        vec[at.k] = own[...]

    @pl.when(at.segment != at.q)
    def _():
        at.copy(own, vec.at[at.k], send.at[0], recv.at[0], at.d, at.partner).wait_recv()

    pair.start()

    @pl.when(at.folded)
    def _():
        mirror.wait_recv()

    @pl.when(jnp.logical_not(at.folded))
    def _():
        vec[2] = own[...]

    pair.wait()
    for t in range(at.chips):
        @pl.when(wanted(t))
        def _():
            to_chip(t).wait_send()

    @pl.when(at.mirror_folded)
    def _():
        mirror.wait_send()


def sum_slices(at, part, other, colsum, cols, rows, total, slots, send, recv):
    states = other.shape[1]
    width = total.shape[2]
    pair = at.copy(
        part.at[:, pl.ds(pl.multiple_of((1 - at.k) * states, 128), states)],
        other, send.at[0], recv.at[0], at.d, at.partner,
    )
    mirror = at.copy(
        part.at[:, pl.ds(2 * states, states)], rows, send.at[1], recv.at[1], at.d, at.mirror
    )
    home = at.copy(
        colsum, cols.at[at.q], send.at[2], recv.at[2 + at.q], at.d, 2 * at.segment + at.k
    )
    pair.start()

    @pl.when(at.folded)
    def _():
        mirror.start()

    keep = jnp.where(at.folded, 0.0, 1.0).astype(jnp.float32)
    for z in range(at.diag_size):
        lanes = slice(2 * states + z * width, 2 * states + (z + 1) * width)
        total[z] = part[:, lanes] * keep
    pair.wait_recv()
    colsum[...] = (
        part[:, pl.ds(pl.multiple_of(at.k * states, 128), states)] + other[...]
    )

    @pl.when(at.segment != at.q)
    def _():
        home.start()

    def add(panel):
        for z in range(at.diag_size):
            total[z] += panel[:, z * width : (z + 1) * width]

    @pl.when(at.segment == at.q)
    def _():
        add(colsum)

    @pl.when(at.mirror_folded)
    def _():
        mirror.wait_recv()
        add(rows)

    for t in range(at.chips):
        @pl.when(jnp.logical_and(at.q != t, at.segment_of(t) == at.q))
        def _():
            at.copy(
                colsum, cols.at[t], send.at[2], recv.at[2 + t], at.d, at.partner
            ).wait_recv()
            add(cols.at[t])

    base = 2 + at.chips
    moves = []
    for o in range(1, at.diag_size):
        peer = (at.d + o) % at.diag_size
        moves.append(
            at.copy(
                total.at[peer], slots.at[o - 1], send.at[2 + o], recv.at[base + o - 1], peer, at.c
            )
        )
        moves[-1].start()
    value = total[at.d]
    for o, move in enumerate(moves):
        move.wait_recv()
        value = value + slots[o]
    for move in moves:
        move.wait_send()
    pair.wait_send()

    @pl.when(at.folded)
    def _():
        mirror.wait_send()

    @pl.when(at.segment != at.q)
    def _():
        home.wait_send()

    return value


def along_diag(at, slots, send, recv):
    moves = []
    for o in range(1, at.diag_size):
        peer = (at.d + o) % at.diag_size
        source = (at.d + at.diag_size - o) % at.diag_size
        out = at.copy(slots.at[at.d], slots.at[at.d], send.at[o - 1], recv.at[o - 1], peer, at.c)
        out.start()
        into = at.copy(
            slots.at[source], slots.at[source], send.at[o - 1], recv.at[o - 1], peer, at.c
        )
        moves.append((out, into))
    return moves


def along_long(at, slots, send, recv):
    moves = []
    for o in range(1, at.long_size):
        peer = (at.c + o) % at.long_size
        source = (at.c + at.long_size - o) % at.long_size
        out = at.copy(slots.at[at.c], slots.at[at.c], send.at[o - 1], recv.at[o - 1], at.d, peer)
        out.start()
        into = at.copy(
            slots.at[source], slots.at[source], send.at[o - 1], recv.at[o - 1], at.d, peer
        )
        moves.append((out, into))
    return moves


def finish(moves):
    for _, into in moves:
        into.wait_recv()
    for out, _ in moves:
        out.wait_send()


def sum_all(at, value, by_diag, by_long, sems):
    by_diag[at.d] = value
    finish(along_diag(at, by_diag, sems[0], sems[1]))
    value = by_diag[0]
    for z in range(1, at.diag_size):
        value = value + by_diag[z]
    by_long[at.c] = value
    finish(along_long(at, by_long, sems[2], sems[3]))
    value = by_long[0]
    for z in range(1, at.long_size):
        value = value + by_long[z]
    return value


def gather_kernel(sizes, x_ref, p_ref, out_ref, own, vec, send, recv):
    at = Place(*sizes)
    at.enter()
    count, states = x_ref.shape
    own[:count] = x_ref[...]
    own[count:] = p_ref[...]
    spread_panels(at, own, vec, send, recv)
    for i in range(3):
        out_ref[:, i * states : (i + 1) * states] = vec[i]


def search_kernel(
    sizes, part, x_ref, slice_ref, search_ref, out_ref,
    other, colsum, cols, rows, total, slots, by_diag, by_long, pieces, own, vec,
    sum_send, sum_recv, z_send, z_recv, l_send, l_recv, s_send, s_recv, g_send, g_recv,
):
    at = Place(*sizes)
    at.enter()
    image = sum_slices(at, part, other, colsum, cols, rows, total, slots, sum_send, sum_recv)
    slice_ref[...] = image
    count, states = x_ref.shape
    width = image.shape[1]
    image = image[:count]
    block = x_ref[:, pl.ds(pl.multiple_of(at.d * width, 128), width)].astype(jnp.float32)
    both = jnp.concatenate([block * image, block * block], 0)
    folded = both[:, :128]
    for i in range(1, width // 128):
        folded = folded + both[:, i * 128 : (i + 1) * 128]
    sums = sum_all(at, folded, by_diag, by_long, (z_send, z_recv, l_send, l_recv))
    sums = jnp.sum(sums, axis=1, keepdims=True)
    quotient = sums[:count] / sums[count:]
    pieces[at.d] = (image - quotient * block).astype(jnp.bfloat16)
    finish(along_diag(at, pieces, s_send, s_recv))
    for z in range(at.diag_size):
        own[:, z * width : (z + 1) * width] = pieces[z]
    spread_panels(at, own, vec, g_send, g_recv)
    search_ref[...] = own[...]
    for i in range(3):
        out_ref[:, i * states : (i + 1) * states] = vec[i]


def project_kernel(
    sizes, part, first_ref, x_ref, search_ref, p_ref, sums_ref, image_ref,
    other, colsum, cols, rows, total, slots, by_diag, by_long, pieces, both,
    sum_send, sum_recv, z_send, z_recv, l_send, l_recv, s_send, s_recv,
):
    at = Place(*sizes)
    at.enter()
    image = sum_slices(at, part, other, colsum, cols, rows, total, slots, sum_send, sum_recv)
    count, width = image.shape
    pieces[at.d] = image
    moves = along_diag(at, pieces, s_send, s_recv)
    lanes = pl.ds(pl.multiple_of(at.d * width, 128), width)
    both[:count] = x_ref[:, lanes].astype(jnp.float32)
    both[count : 2 * count] = search_ref[:, lanes].astype(jnp.float32)
    both[2 * count : 3 * count] = p_ref[:, lanes].astype(jnp.float32)
    both[3 * count : 4 * count] = first_ref[:count]
    both[4 * count : 5 * count] = image
    both[5 * count : 6 * count] = first_ref[count:]
    both[6 * count :] = jnp.zeros((both.shape[0] - 6 * count, width), jnp.float32)
    value = lax.dot_general(
        both[: 3 * count], both[...], (((1,), (1,)), ((), ())),
        precision=HIGHEST, preferred_element_type=jnp.float32,
    )
    sums_ref[...] = sum_all(at, value, by_diag, by_long, (z_send, z_recv, l_send, l_recv))
    finish(moves)
    for z in range(at.diag_size):
        image_ref[:, z * width : (z + 1) * width] = pieces[z]


def sum_scratch(count, states, diag_size, long_size):
    width = states // diag_size
    f32 = jnp.float32
    return [
        pltpu.VMEM((count, states), f32),
        pltpu.VMEM((count, states), f32),
        pltpu.VMEM((long_size // 2, count, states), f32),
        pltpu.VMEM((count, states), f32),
        pltpu.VMEM((diag_size, count, width), f32),
        pltpu.VMEM((diag_size - 1, count, width), f32),
    ]


def remote_call(kernel, sizes, collective, outs, scratch, *args):
    vmem = pl.BlockSpec(memory_space=pltpu.VMEM)
    return pl.pallas_call(
        functools.partial(kernel, sizes),
        in_specs=[vmem] * len(args),
        out_specs=[vmem] * len(outs),
        out_shape=[jax.ShapeDtypeStruct(*o) for o in outs],
        scratch_shapes=scratch,
        compiler_params=pltpu.CompilerParams(
            collective_id=collective, has_side_effects=True, vmem_limit_bytes=40 << 20
        ),
    )(*args)


def local(tiles, tile_rows, tile_cols, tile_counts, block_x, block_p):
    tile_block = tiles[0, 0]
    rows = tile_rows[0, 0]
    cols = tile_cols[0, 0]
    edge = tile_block.shape[-1]
    count, states = block_x.shape
    panel_tiles = states // edge
    diag_index = lax.axis_index("diag")
    long_index = lax.axis_index("long")
    long_size = lax.axis_size("long")
    diag_size = lax.axis_size("diag")
    folded = long_index < 2 * diag_index
    row_panel = jnp.where(folded, long_size - 1 - long_index, long_index)
    segment_id = jnp.where(folded, diag_size - 1 - diag_index, diag_index)
    meta = jnp.stack(
        [tile_counts[0, 0], row_panel * panel_tiles, 2 * segment_id * panel_tiles]
    ).astype(jnp.int32)
    sizes = (diag_size, long_size)
    width = states // diag_size
    chips = long_size // 2
    f32, bf16, dma = jnp.float32, jnp.bfloat16, pltpu.SemaphoreType.DMA
    spread_sems = [dma((chips + 2,)), dma((3,))]
    sum_sems = [dma((diag_size + 2,)), dma((1 + chips + diag_size,))]
    all_sems = [dma((n - 1,)) for n in (diag_size, diag_size, long_size, long_size)]
    diag_sems = [dma((diag_size - 1,))] * 2

    vectors = remote_call(
        gather_kernel, sizes, 1, [((2 * count, 3 * states), bf16)],
        [pltpu.VMEM((2 * count, states), bf16), pltpu.VMEM((3, 2 * count, states), bf16)]
        + spread_sems,
        block_x, block_p,
    )[0]
    part = apply_tiles(tile_block, rows, cols, meta, vectors)
    first, search, vectors = remote_call(
        search_kernel, sizes, 2,
        [((2 * count, width), f32), ((count, states), bf16), ((count, 3 * states), bf16)],
        sum_scratch(2 * count, states, *sizes)
        + [
            pltpu.VMEM((diag_size, 2 * count, 128), f32),
            pltpu.VMEM((long_size, 2 * count, 128), f32),
            pltpu.VMEM((diag_size, count, width), bf16),
            pltpu.VMEM((count, states), bf16),
            pltpu.VMEM((3, count, states), bf16),
        ]
        + sum_sems + all_sems + diag_sems + spread_sems,
        part, block_x,
    )
    first_whole = lax.all_gather(first, "diag", axis=1, tiled=True)
    part = apply_tiles(tile_block, rows, cols, meta, vectors)
    sums, image_w = remote_call(
        project_kernel, sizes, 3,
        [((3 * count, 128), f32), ((count, states), f32)],
        sum_scratch(count, states, *sizes)
        + [
            pltpu.VMEM((diag_size, 3 * count, 128), f32),
            pltpu.VMEM((long_size, 3 * count, 128), f32),
            pltpu.VMEM((diag_size, count, width), f32),
            pltpu.VMEM((128, width), f32),
        ]
        + sum_sems + all_sems + diag_sems,
        part, first, block_x, search, block_p,
    )
    basis_in = jnp.concatenate([block_x, search, block_p], 0)
    himage = jnp.concatenate([first_whole[:count], image_w, first_whole[count:]], 0)
    return tuple(ritz(sums, basis_in, himage))


def solution(mesh):
    return jax.shard_map(
        local,
        mesh=mesh,
        in_specs=(
            P("diag", "long", None, None, None),
            P("diag", "long", None),
            P("diag", "long", None),
            P("diag", "long"),
            P(None, "long"),
            P(None, "long"),
        ),
        out_specs=(P(None, "long"), P(None, "long"), P()),
        check_vma=False,
    )
```

```python
import functools

import jax
import jax.numpy as jnp
from jax import lax
from jax.experimental import pallas as pl
from jax.experimental.pallas import tpu as pltpu
from jax.sharding import PartitionSpec as P

HIGHEST = lax.Precision.HIGHEST
STEP = 64
UNROLL = 32


def tile_kernel(rows_ref, cols_ref, meta_ref, vec_ref, tile_ref, out_ref):
    edge = tile_ref.shape[-1]
    row_lane = out_ref.shape[1] // 3 * 2
    base = pl.program_id(0) * STEP

    @pl.when(pl.program_id(0) == 0)
    def _():
        out_ref[...] = jnp.zeros_like(out_ref)

    count, row_off, col_off = meta_ref[0], meta_ref[1], meta_ref[2]
    live = jnp.clip(count - base, 0, STEP)

    count_vec = vec_ref.shape[0]
    blank = jnp.zeros((count_vec, edge), vec_ref.dtype)

    def spot(k):
        row = rows_ref[base + k]
        col = cols_ref[base + k]
        weight = jnp.where(row + row_off == col + col_off, 0.5, 1.0).astype(jnp.float32)
        weight = jnp.where(base + k < count, weight, 0.0)
        row_at = pl.ds(pl.multiple_of(row * edge + row_lane, edge), edge)
        col_at = pl.ds(pl.multiple_of(col * edge, edge), edge)
        return row_at, col_at, weight

    def group(i, carry):
        found = []
        for u in range(0, UNROLL, 2):
            k = i * UNROLL + u
            row_a, col_a, weight_a = spot(k)
            row_b, col_b, weight_b = spot(k + 1)
            two = tile_ref[pl.ds(k, 2)].reshape(2 * edge, edge)
            forward = lax.dot_general(
                jnp.concatenate([vec_ref[:, col_a], vec_ref[:, col_b]], 0),
                two,
                (((1,), (1,)), ((), ())),
                preferred_element_type=jnp.float32,
            )
            upper = jnp.concatenate([vec_ref[:, row_a], blank], 1)
            lower = jnp.concatenate([blank, vec_ref[:, row_b]], 1)
            backward = jnp.dot(
                jnp.concatenate([upper, lower], 0), two, preferred_element_type=jnp.float32
            )
            found.append(
                (row_a, col_a, forward[:count_vec, :edge] * weight_a, backward[:count_vec] * weight_a)
            )
            found.append(
                (row_b, col_b, forward[count_vec:, edge:] * weight_b, backward[count_vec:] * weight_b)
            )
        for row_at, col_at, forward, backward in found:
            out_ref[:, row_at] += forward
            out_ref[:, col_at] += backward
        return carry

    lax.fori_loop(0, (live + UNROLL - 1) // UNROLL, group, 0)


def apply_tiles(tiles, rows, cols, meta, vectors):
    slots, edge = tiles.shape[0], tiles.shape[-1]
    width, states = vectors.shape
    smem = pl.BlockSpec(memory_space=pltpu.SMEM)
    return pl.pallas_call(
        tile_kernel,
        grid=(slots // STEP,),
        in_specs=[
            smem,
            smem,
            smem,
            pl.BlockSpec(memory_space=pltpu.VMEM),
            pl.BlockSpec((STEP, edge, edge), lambda i: (i, 0, 0)),
        ],
        out_specs=pl.BlockSpec((width, states), lambda i: (0, 0)),
        out_shape=jax.ShapeDtypeStruct((width, states), jnp.float32),
        compiler_params=pltpu.CompilerParams(vmem_limit_bytes=40 << 20),
        cost_estimate=pl.CostEstimate(
            flops=4 * slots * edge * edge * width,
            bytes_accessed=2 * slots * edge * edge,
            transcendentals=0,
        ),
    )(rows, cols, meta, vectors, tiles)


def ritz_kernel(sums_ref, basis_ref, image_ref, rb_ref, ri_ref, rm_ref):
    size = sums_ref.shape[0]
    lane = lax.broadcasted_iota(jnp.int32, (size, size), 1)
    row = lax.broadcasted_iota(jnp.int32, (size, size), 0)
    below = lax.broadcasted_iota(jnp.int32, (size, 1), 0)
    sums = sums_ref[...]
    left = sums[:, :size]
    right = jnp.where(lane == row, 1.0, 0.0).astype(jnp.float32)
    pivots = jnp.zeros((size, 1), jnp.float32)
    for k in range(size):
        pivot = left[k : k + 1, k : k + 1]
        pivots = jnp.where(below == k, pivot, pivots)
        scale = jnp.where(below > k, left[:, k : k + 1] * (1.0 / pivot), 0.0)
        left_row, right_row = left[k : k + 1, :], right[k : k + 1, :]
        left = left - scale * left_row
        right = right - scale * right_row
    inverse = right * (1.0 / jnp.sqrt(pivots))
    nt = (((1,), (1,)), ((), ()))
    half = jnp.dot(inverse, sums[:, size : 2 * size], precision=HIGHEST, preferred_element_type=jnp.float32)
    one = lax.dot_general(half, inverse, nt, precision=HIGHEST, preferred_element_type=jnp.float32)
    two = lax.dot_general(inverse, half, nt, precision=HIGHEST, preferred_element_type=jnp.float32)
    rm_ref[...] = 0.5 * (one + two)
    rb_ref[...] = jnp.dot(
        inverse, basis_ref[...].astype(jnp.float32), precision=HIGHEST, preferred_element_type=jnp.float32
    )
    ri_ref[...] = jnp.dot(
        inverse, image_ref[...], precision=HIGHEST, preferred_element_type=jnp.float32
    )


def ritz(sums, basis, image):
    vmem = pl.BlockSpec(memory_space=pltpu.VMEM)
    like = jax.ShapeDtypeStruct(image.shape, jnp.float32)
    return pl.pallas_call(
        ritz_kernel,
        in_specs=[vmem] * 3,
        out_specs=[vmem] * 3,
        out_shape=[like, like, jax.ShapeDtypeStruct((sums.shape[0], sums.shape[0]), jnp.float32)],
        compiler_params=pltpu.CompilerParams(vmem_limit_bytes=40 << 20),
    )(sums, basis, image)


class Place:
    def __init__(self, diag_size, long_size):
        self.diag_size, self.long_size = diag_size, long_size
        self.chips = long_size // 2
        self.d = lax.axis_index("diag")
        self.c = lax.axis_index("long")
        self.q, self.k = self.c // 2, self.c % 2
        self.partner = self.q * 2 + 1 - self.k
        self.mirror = long_size - 1 - self.c
        self.folded = self.q < self.d
        self.segment = self.segment_of(self.q)
        self.mirror_folded = self.mirror // 2 < self.d

    def segment_of(self, chip):
        return jnp.where(chip < self.d, self.diag_size - 1 - self.d, self.d)

    def copy(self, src, dst, send, recv, d, c):
        return pltpu.make_async_remote_copy(
            src_ref=src,
            dst_ref=dst,
            send_sem=send,
            recv_sem=recv,
            device_id=(d, c),
            device_id_type=pl.DeviceIdType.MESH,
        )

    def enter(self):
        barrier = pltpu.get_barrier_semaphore()
        peers = [(self.d, (self.c + o) % self.long_size) for o in range(1, self.long_size)]
        peers += [((self.d + o) % self.diag_size, self.c) for o in range(1, self.diag_size)]
        for peer in peers:
            pl.semaphore_signal(barrier, inc=1, device_id=peer, device_id_type=pl.DeviceIdType.MESH)
        pl.semaphore_wait(barrier, len(peers))


def spread_panels(at, own, vec, send, recv):
    def to_chip(t):
        return at.copy(own, vec.at[at.k], send.at[t], recv.at[0], at.d, 2 * t + at.k)

    def wanted(t):
        return jnp.logical_and(at.q != t, at.segment_of(t) == at.q)

    mirror = at.copy(own, vec.at[2], send.at[at.chips], recv.at[1], at.d, at.mirror)
    for t in range(at.chips):
        @pl.when(wanted(t))
        def _():
            to_chip(t).start()

    @pl.when(at.mirror_folded)
    def _():
        mirror.start()

    pair = at.copy(
        vec.at[at.k], vec.at[at.k], send.at[at.chips + 1], recv.at[2], at.d, at.partner
    )

    @pl.when(at.segment == at.q)
    def _():
        vec[at.k] = own[...]

    @pl.when(at.segment != at.q)
    def _():
        at.copy(own, vec.at[at.k], send.at[0], recv.at[0], at.d, at.partner).wait_recv()

    pair.start()

    @pl.when(at.folded)
    def _():
        mirror.wait_recv()

    @pl.when(jnp.logical_not(at.folded))
    def _():
        vec[2] = own[...]

    pair.wait()
    for t in range(at.chips):
        @pl.when(wanted(t))
        def _():
            to_chip(t).wait_send()

    @pl.when(at.mirror_folded)
    def _():
        mirror.wait_send()


class PanelSum:
    def __init__(self, at, part, lo, hi, bufs, send, recv):
        self.at, self.part, self.lo, self.hi = at, part, lo, hi
        self.other, self.colsum, self.cols, self.rows, self.total, self.slots = bufs
        self.send, self.recv = send, recv
        self.states, self.width = self.other.shape[1], self.total.shape[2]
        states = self.states
        self.mine = pl.ds(pl.multiple_of(at.k * states, 128), states)
        theirs = pl.ds(pl.multiple_of((1 - at.k) * states, 128), states)
        self.pair = at.copy(
            part.at[lo:hi, theirs], self.other, send.at[0], recv.at[0], at.d, at.partner
        )
        self.mirror = at.copy(
            part.at[lo:hi, pl.ds(2 * states, states)],
            self.rows, send.at[1], recv.at[1], at.d, at.mirror,
        )
        self.home = at.copy(
            self.colsum, self.cols.at[at.q], send.at[2], recv.at[2 + at.q],
            at.d, 2 * at.segment + at.k,
        )

    def start(self):
        self.pair.start()

        @pl.when(self.at.folded)
        def _():
            self.mirror.start()

    def columns(self):
        at = self.at
        self.pair.wait_recv()
        self.colsum[...] = self.part[self.lo : self.hi, self.mine] + self.other[...]

        @pl.when(at.segment != at.q)
        def _():
            self.home.start()

    def add(self, panel):
        width = self.width
        for z in range(self.at.diag_size):
            self.total[z] += panel[:, z * width : (z + 1) * width]

    def totals(self):
        at, width = self.at, self.width
        keep = jnp.where(at.folded, 0.0, 1.0).astype(jnp.float32)
        for z in range(at.diag_size):
            lanes = slice(2 * self.states + z * width, 2 * self.states + (z + 1) * width)
            self.total[z] = self.part[self.lo : self.hi, lanes] * keep

        @pl.when(at.segment == at.q)
        def _():
            self.add(self.colsum)

        @pl.when(at.mirror_folded)
        def _():
            self.mirror.wait_recv()
            self.add(self.rows)

        for t in range(at.chips):
            @pl.when(jnp.logical_and(at.q != t, at.segment_of(t) == at.q))
            def _():
                at.copy(
                    self.colsum, self.cols.at[t], self.send.at[2], self.recv.at[2 + t],
                    at.d, at.partner,
                ).wait_recv()
                self.add(self.cols.at[t])

        base = 2 + at.chips
        self.moves = []
        for o in range(1, at.diag_size):
            peer = (at.d + o) % at.diag_size
            self.moves.append(
                at.copy(
                    self.total.at[peer], self.slots.at[o - 1],
                    self.send.at[2 + o], self.recv.at[base + o - 1], peer, at.c,
                )
            )
            self.moves[-1].start()

    def result(self):
        value = self.total[self.at.d]
        for o, move in enumerate(self.moves):
            move.wait_recv()
            value = value + self.slots[o]
        return value

    def close(self):
        for move in self.moves:
            move.wait_send()
        self.pair.wait_send()

        @pl.when(self.at.folded)
        def _():
            self.mirror.wait_send()

        @pl.when(self.at.segment != self.at.q)
        def _():
            self.home.wait_send()


def along_diag(at, slots, send, recv):
    moves = []
    for o in range(1, at.diag_size):
        peer = (at.d + o) % at.diag_size
        source = (at.d + at.diag_size - o) % at.diag_size
        out = at.copy(slots.at[at.d], slots.at[at.d], send.at[o - 1], recv.at[o - 1], peer, at.c)
        out.start()
        into = at.copy(
            slots.at[source], slots.at[source], send.at[o - 1], recv.at[o - 1], peer, at.c
        )
        moves.append((out, into))
    return moves


def along_long(at, slots, send, recv):
    moves = []
    for o in range(1, at.long_size):
        peer = (at.c + o) % at.long_size
        source = (at.c + at.long_size - o) % at.long_size
        out = at.copy(slots.at[at.c], slots.at[at.c], send.at[o - 1], recv.at[o - 1], at.d, peer)
        out.start()
        into = at.copy(
            slots.at[source], slots.at[source], send.at[o - 1], recv.at[o - 1], at.d, peer
        )
        moves.append((out, into))
    return moves


def finish(moves):
    for _, into in moves:
        into.wait_recv()
    for out, _ in moves:
        out.wait_send()


def sum_all(at, value, by_diag, by_long, sems):
    by_diag[at.d] = value
    finish(along_diag(at, by_diag, sems[0], sems[1]))
    value = by_diag[0]
    for z in range(1, at.diag_size):
        value = value + by_diag[z]
    by_long[at.c] = value
    finish(along_long(at, by_long, sems[2], sems[3]))
    value = by_long[0]
    for z in range(1, at.long_size):
        value = value + by_long[z]
    return value


def gather_kernel(sizes, x_ref, p_ref, out_ref, own, vec, send, recv):
    at = Place(*sizes)
    at.enter()
    count, states = x_ref.shape
    own[:count] = x_ref[...]
    own[count:] = p_ref[...]
    spread_panels(at, own, vec, send, recv)
    for i in range(3):
        out_ref[:, i * states : (i + 1) * states] = vec[i]


def search_kernel(sizes, part, x_ref, slice_ref, search_ref, out_ref, *scratch):
    bufs_x, bufs_p = scratch[:6], scratch[6:12]
    by_diag, by_long, pieces, own, vec = scratch[12:17]
    send_x, recv_x, send_p, recv_p = scratch[17:21]
    sums_sems, s_send, s_recv, g_send, g_recv = scratch[21:25], *scratch[25:29]
    at = Place(*sizes)
    at.enter()
    count, states = x_ref.shape
    sum_x = PanelSum(at, part, 0, count, bufs_x, send_x, recv_x)
    sum_p = PanelSum(at, part, count, 2 * count, bufs_p, send_p, recv_p)
    sum_x.start()
    sum_x.columns()
    sum_p.start()
    sum_x.totals()
    sum_p.columns()
    image = sum_x.result()
    slice_ref[:count] = image
    width = image.shape[1]
    block = x_ref[:, pl.ds(pl.multiple_of(at.d * width, 128), width)].astype(jnp.float32)
    both = jnp.concatenate([block * image, block * block], 0)
    folded = both[:, :128]
    for i in range(1, width // 128):
        folded = folded + both[:, i * 128 : (i + 1) * 128]
    sums = sum_all(at, folded, by_diag, by_long, sums_sems)
    sums = jnp.sum(sums, axis=1, keepdims=True)
    quotient = sums[:count] / sums[count:]
    pieces[at.d] = (image - quotient * block).astype(jnp.bfloat16)
    moves = along_diag(at, pieces, s_send, s_recv)
    sum_p.totals()
    finish(moves)
    for z in range(at.diag_size):
        own[:, z * width : (z + 1) * width] = pieces[z]
    spread_panels(at, own, vec, g_send, g_recv)
    search_ref[...] = own[...]
    for i in range(3):
        out_ref[:, i * states : (i + 1) * states] = vec[i]
    slice_ref[count:] = sum_p.result()
    sum_x.close()
    sum_p.close()


def project_kernel(
    sizes, part, first_ref, x_ref, search_ref, p_ref, sums_ref, image_ref,
    other, colsum, cols, rows, total, slots, by_diag, by_long, pieces, firsts, both,
    sum_send, sum_recv, z_send, z_recv, l_send, l_recv, s_send, s_recv, f_send, f_recv,
):
    at = Place(*sizes)
    at.enter()
    bufs = (other, colsum, cols, rows, total, slots)
    count = x_ref.shape[0]
    sum_w = PanelSum(at, part, 0, count, bufs, sum_send, sum_recv)
    sum_w.start()
    firsts[at.d] = first_ref[...]
    first_moves = along_diag(at, firsts, f_send, f_recv)
    sum_w.columns()
    sum_w.totals()
    image = sum_w.result()
    width = image.shape[1]
    pieces[at.d] = image
    moves = along_diag(at, pieces, s_send, s_recv)
    lanes = pl.ds(pl.multiple_of(at.d * width, 128), width)
    both[:count] = x_ref[:, lanes].astype(jnp.float32)
    both[count : 2 * count] = search_ref[:, lanes].astype(jnp.float32)
    both[2 * count : 3 * count] = p_ref[:, lanes].astype(jnp.float32)
    both[3 * count : 4 * count] = first_ref[:count]
    both[4 * count : 5 * count] = image
    both[5 * count : 6 * count] = first_ref[count:]
    both[6 * count :] = jnp.zeros((both.shape[0] - 6 * count, width), jnp.float32)
    value = lax.dot_general(
        both[: 3 * count], both[...], (((1,), (1,)), ((), ())),
        precision=HIGHEST, preferred_element_type=jnp.float32,
    )
    sums_ref[...] = sum_all(at, value, by_diag, by_long, (z_send, z_recv, l_send, l_recv))
    finish(moves)
    finish(first_moves)
    for z in range(at.diag_size):
        lanes = slice(z * width, (z + 1) * width)
        image_ref[:count, lanes] = firsts[z, :count]
        image_ref[count : 2 * count, lanes] = pieces[z]
        image_ref[2 * count :, lanes] = firsts[z, count:]
    sum_w.close()


def sum_scratch(count, states, diag_size, long_size):
    width = states // diag_size
    f32 = jnp.float32
    return [
        pltpu.VMEM((count, states), f32),
        pltpu.VMEM((count, states), f32),
        pltpu.VMEM((long_size // 2, count, states), f32),
        pltpu.VMEM((count, states), f32),
        pltpu.VMEM((diag_size, count, width), f32),
        pltpu.VMEM((diag_size - 1, count, width), f32),
    ]


def remote_call(kernel, sizes, collective, outs, scratch, *args):
    vmem = pl.BlockSpec(memory_space=pltpu.VMEM)
    return pl.pallas_call(
        functools.partial(kernel, sizes),
        in_specs=[vmem] * len(args),
        out_specs=[vmem] * len(outs),
        out_shape=[jax.ShapeDtypeStruct(*o) for o in outs],
        scratch_shapes=scratch,
        compiler_params=pltpu.CompilerParams(
            collective_id=collective, has_side_effects=True, vmem_limit_bytes=40 << 20
        ),
    )(*args)


def local(tiles, tile_rows, tile_cols, tile_counts, block_x, block_p):
    tile_block = tiles[0, 0]
    rows = tile_rows[0, 0]
    cols = tile_cols[0, 0]
    edge = tile_block.shape[-1]
    count, states = block_x.shape
    panel_tiles = states // edge
    diag_index = lax.axis_index("diag")
    long_index = lax.axis_index("long")
    long_size = lax.axis_size("long")
    diag_size = lax.axis_size("diag")
    folded = long_index < 2 * diag_index
    row_panel = jnp.where(folded, long_size - 1 - long_index, long_index)
    segment_id = jnp.where(folded, diag_size - 1 - diag_index, diag_index)
    meta = jnp.stack(
        [tile_counts[0, 0], row_panel * panel_tiles, 2 * segment_id * panel_tiles]
    ).astype(jnp.int32)
    sizes = (diag_size, long_size)
    width = states // diag_size
    chips = long_size // 2
    f32, bf16, dma = jnp.float32, jnp.bfloat16, pltpu.SemaphoreType.DMA
    spread_sems = [dma((chips + 2,)), dma((3,))]
    sum_sems = [dma((diag_size + 2,)), dma((1 + chips + diag_size,))]
    all_sems = [dma((n - 1,)) for n in (diag_size, diag_size, long_size, long_size)]
    diag_sems = [dma((diag_size - 1,))] * 2

    vectors = remote_call(
        gather_kernel, sizes, 1, [((2 * count, 3 * states), bf16)],
        [pltpu.VMEM((2 * count, states), bf16), pltpu.VMEM((3, 2 * count, states), bf16)]
        + spread_sems,
        block_x, block_p,
    )[0]
    part = apply_tiles(tile_block, rows, cols, meta, vectors)
    first, search, vectors = remote_call(
        search_kernel, sizes, 2,
        [((2 * count, width), f32), ((count, states), bf16), ((count, 3 * states), bf16)],
        sum_scratch(count, states, *sizes) * 2
        + [
            pltpu.VMEM((diag_size, 2 * count, 128), f32),
            pltpu.VMEM((long_size, 2 * count, 128), f32),
            pltpu.VMEM((diag_size, count, width), bf16),
            pltpu.VMEM((count, states), bf16),
            pltpu.VMEM((3, count, states), bf16),
        ]
        + sum_sems * 2 + all_sems + diag_sems + spread_sems,
        part, block_x,
    )
    part = apply_tiles(tile_block, rows, cols, meta, vectors)
    sums, himage = remote_call(
        project_kernel, sizes, 3,
        [((3 * count, 128), f32), ((3 * count, states), f32)],
        sum_scratch(count, states, *sizes)
        + [
            pltpu.VMEM((diag_size, 3 * count, 128), f32),
            pltpu.VMEM((long_size, 3 * count, 128), f32),
            pltpu.VMEM((diag_size, count, width), f32),
            pltpu.VMEM((diag_size, 2 * count, width), f32),
            pltpu.VMEM((128, width), f32),
        ]
        + sum_sems + all_sems + diag_sems * 2,
        part, first, block_x, search, block_p,
    )
    basis_in = jnp.concatenate([block_x, search, block_p], 0)
    return tuple(ritz(sums, basis_in, himage))


def solution(mesh):
    return jax.shard_map(
        local,
        mesh=mesh,
        in_specs=(
            P("diag", "long", None, None, None),
            P("diag", "long", None),
            P("diag", "long", None),
            P("diag", "long"),
            P(None, "long"),
            P(None, "long"),
        ),
        out_specs=(P(None, "long"), P(None, "long"), P()),
        check_vma=False,
    )
```

```python
import functools

import jax
import jax.numpy as jnp
from jax import lax
from jax.experimental import pallas as pl
from jax.experimental.pallas import tpu as pltpu
from jax.sharding import PartitionSpec as P

HIGHEST = lax.Precision.HIGHEST
STEP = 64
UNROLL = 32


def tile_kernel(rows_ref, cols_ref, meta_ref, vec_ref, tile_ref, out_ref):
    edge = tile_ref.shape[-1]
    row_lane = out_ref.shape[1] // 3 * 2
    base = pl.program_id(0) * STEP

    @pl.when(pl.program_id(0) == 0)
    def _():
        out_ref[...] = jnp.zeros_like(out_ref)

    count, row_off, col_off = meta_ref[0], meta_ref[1], meta_ref[2]
    live = jnp.clip(count - base, 0, STEP)

    count_vec = vec_ref.shape[0]
    blank = jnp.zeros((count_vec, edge), vec_ref.dtype)

    def spot(k):
        row = rows_ref[base + k]
        col = cols_ref[base + k]
        weight = jnp.where(row + row_off == col + col_off, 0.5, 1.0).astype(jnp.float32)
        weight = jnp.where(base + k < count, weight, 0.0)
        row_at = pl.ds(pl.multiple_of(row * edge + row_lane, edge), edge)
        col_at = pl.ds(pl.multiple_of(col * edge, edge), edge)
        return row_at, col_at, weight

    def group(i, carry):
        found = []
        for u in range(0, UNROLL, 2):
            k = i * UNROLL + u
            row_a, col_a, weight_a = spot(k)
            row_b, col_b, weight_b = spot(k + 1)
            two = tile_ref[pl.ds(k, 2)].reshape(2 * edge, edge)
            forward = lax.dot_general(
                jnp.concatenate([vec_ref[:, col_a], vec_ref[:, col_b]], 0),
                two,
                (((1,), (1,)), ((), ())),
                preferred_element_type=jnp.float32,
            )
            upper = jnp.concatenate([vec_ref[:, row_a], blank], 1)
            lower = jnp.concatenate([blank, vec_ref[:, row_b]], 1)
            backward = jnp.dot(
                jnp.concatenate([upper, lower], 0), two, preferred_element_type=jnp.float32
            )
            found.append(
                (row_a, col_a, forward[:count_vec, :edge] * weight_a, backward[:count_vec] * weight_a)
            )
            found.append(
                (row_b, col_b, forward[count_vec:, edge:] * weight_b, backward[count_vec:] * weight_b)
            )
        for row_at, col_at, forward, backward in found:
            out_ref[:, row_at] += forward
            out_ref[:, col_at] += backward
        return carry

    lax.fori_loop(0, (live + UNROLL - 1) // UNROLL, group, 0)


def apply_tiles(tiles, rows, cols, meta, vectors):
    slots, edge = tiles.shape[0], tiles.shape[-1]
    width, states = vectors.shape
    smem = pl.BlockSpec(memory_space=pltpu.SMEM)
    return pl.pallas_call(
        tile_kernel,
        grid=(slots // STEP,),
        in_specs=[
            smem,
            smem,
            smem,
            pl.BlockSpec(memory_space=pltpu.VMEM),
            pl.BlockSpec((STEP, edge, edge), lambda i: (i, 0, 0)),
        ],
        out_specs=pl.BlockSpec((width, states), lambda i: (0, 0)),
        out_shape=jax.ShapeDtypeStruct((width, states), jnp.float32),
        compiler_params=pltpu.CompilerParams(vmem_limit_bytes=40 << 20),
        cost_estimate=pl.CostEstimate(
            flops=4 * slots * edge * edge * width,
            bytes_accessed=2 * slots * edge * edge,
            transcendentals=0,
        ),
    )(rows, cols, meta, vectors, tiles)


def ritz_kernel(sums_ref, basis_ref, image_ref, rb_ref, ri_ref, rm_ref):
    size = sums_ref.shape[0]
    lane = lax.broadcasted_iota(jnp.int32, (size, size), 1)
    row = lax.broadcasted_iota(jnp.int32, (size, size), 0)
    below = lax.broadcasted_iota(jnp.int32, (size, 1), 0)
    sums = sums_ref[...]
    left = sums[:, :size]
    right = jnp.where(lane == row, 1.0, 0.0).astype(jnp.float32)
    pivots = jnp.zeros((size, 1), jnp.float32)
    for k in range(size):
        pivot = left[k : k + 1, k : k + 1]
        pivots = jnp.where(below == k, pivot, pivots)
        scale = jnp.where(below > k, left[:, k : k + 1] * (1.0 / pivot), 0.0)
        left_row, right_row = left[k : k + 1, :], right[k : k + 1, :]
        left = left - scale * left_row
        right = right - scale * right_row
    inverse = right * (1.0 / jnp.sqrt(pivots))
    nt = (((1,), (1,)), ((), ()))
    half = jnp.dot(inverse, sums[:, size : 2 * size], precision=HIGHEST, preferred_element_type=jnp.float32)
    one = lax.dot_general(half, inverse, nt, precision=HIGHEST, preferred_element_type=jnp.float32)
    two = lax.dot_general(inverse, half, nt, precision=HIGHEST, preferred_element_type=jnp.float32)
    rm_ref[...] = 0.5 * (one + two)
    rb_ref[...] = jnp.dot(
        inverse, basis_ref[...].astype(jnp.float32), precision=HIGHEST, preferred_element_type=jnp.float32
    )
    ri_ref[...] = jnp.dot(
        inverse, image_ref[...], precision=HIGHEST, preferred_element_type=jnp.float32
    )


def ritz(sums, basis, image):
    vmem = pl.BlockSpec(memory_space=pltpu.VMEM)
    like = jax.ShapeDtypeStruct(image.shape, jnp.float32)
    return pl.pallas_call(
        ritz_kernel,
        in_specs=[vmem] * 3,
        out_specs=[vmem] * 3,
        out_shape=[like, like, jax.ShapeDtypeStruct((sums.shape[0], sums.shape[0]), jnp.float32)],
        compiler_params=pltpu.CompilerParams(vmem_limit_bytes=40 << 20),
    )(sums, basis, image)


class Place:
    def __init__(self, diag_size, long_size):
        self.diag_size, self.long_size = diag_size, long_size
        self.chips = long_size // 2
        self.d = lax.axis_index("diag")
        self.c = lax.axis_index("long")
        self.q, self.k = self.c // 2, self.c % 2
        self.partner = self.q * 2 + 1 - self.k
        self.mirror = long_size - 1 - self.c
        self.folded = self.q < self.d
        self.segment = self.segment_of(self.q)
        self.mirror_folded = self.mirror // 2 < self.d

    def segment_of(self, chip):
        return jnp.where(chip < self.d, self.diag_size - 1 - self.d, self.d)

    def copy(self, src, dst, send, recv, d, c):
        return pltpu.make_async_remote_copy(
            src_ref=src,
            dst_ref=dst,
            send_sem=send,
            recv_sem=recv,
            device_id=(d, c),
            device_id_type=pl.DeviceIdType.MESH,
        )

    def enter(self):
        barrier = pltpu.get_barrier_semaphore()
        peers = [(self.d, (self.c + o) % self.long_size) for o in range(1, self.long_size)]
        peers += [((self.d + o) % self.diag_size, self.c) for o in range(1, self.diag_size)]
        for peer in peers:
            pl.semaphore_signal(barrier, inc=1, device_id=peer, device_id_type=pl.DeviceIdType.MESH)
        pl.semaphore_wait(barrier, len(peers))


def spread_panels(at, own, vec, send, recv):
    def to_chip(t):
        return at.copy(own, vec.at[at.k], send.at[t], recv.at[0], at.d, 2 * t + at.k)

    def wanted(t):
        return jnp.logical_and(at.q != t, at.segment_of(t) == at.q)

    mirror = at.copy(own, vec.at[2], send.at[at.chips], recv.at[1], at.d, at.mirror)
    for t in range(at.chips):
        @pl.when(wanted(t))
        def _():
            to_chip(t).start()

    @pl.when(at.mirror_folded)
    def _():
        mirror.start()

    pair = at.copy(
        vec.at[at.k], vec.at[at.k], send.at[at.chips + 1], recv.at[2], at.d, at.partner
    )

    @pl.when(at.segment == at.q)
    def _():
        vec[at.k] = own[...]

    @pl.when(at.segment != at.q)
    def _():
        at.copy(own, vec.at[at.k], send.at[0], recv.at[0], at.d, at.partner).wait_recv()

    pair.start()

    @pl.when(at.folded)
    def _():
        mirror.wait_recv()

    @pl.when(jnp.logical_not(at.folded))
    def _():
        vec[2] = own[...]

    pair.wait()
    for t in range(at.chips):
        @pl.when(wanted(t))
        def _():
            to_chip(t).wait_send()

    @pl.when(at.mirror_folded)
    def _():
        mirror.wait_send()


class PanelSum:
    def __init__(self, at, part, lo, hi, bufs, send, recv):
        self.at, self.part, self.lo, self.hi = at, part, lo, hi
        self.other, self.colsum, self.cols, self.rows, self.total, self.slots = bufs
        self.send, self.recv = send, recv
        size = at.diag_size
        self.width = self.total.shape[2]
        self.states = self.width * size
        self.order = [(o, (at.d + o) % size) for o in [*range(1, size), 0]]

    def lanes(self, panel, z):
        start = pl.multiple_of(panel * self.states + z * self.width, 128)
        return pl.ds(start, self.width)

    def pair(self, o, z):
        at = self.at
        return at.copy(
            self.part.at[self.lo : self.hi, self.lanes(1 - at.k, z)], self.other.at[z],
            self.send.at[o], self.recv.at[o], at.d, at.partner,
        )

    def mirror(self, o, z):
        at, size = self.at, self.at.diag_size
        return at.copy(
            self.part.at[self.lo : self.hi, self.lanes(2, z)], self.rows.at[z],
            self.send.at[size + o], self.recv.at[size + o], at.d, at.mirror,
        )

    def home(self, o, z, slot, chip):
        at, size = self.at, self.at.diag_size
        return at.copy(
            self.colsum.at[z], self.cols.at[slot, z],
            self.send.at[2 * size + o], self.recv.at[(2 + slot) * size + o],
            at.d, chip,
        )

    def move(self, o, z):
        at, size = self.at, self.at.diag_size
        return at.copy(
            self.total.at[z], self.slots.at[o - 1],
            self.send.at[3 * size + o - 1], self.recv.at[(2 + at.chips) * size + o - 1], z, at.c,
        )

    def start(self):
        for o, z in self.order:
            self.pair(o, z).start()

            @pl.when(self.at.folded)
            def _():
                self.mirror(o, z).start()

    def columns(self):
        at = self.at
        for o, z in self.order:
            self.pair(o, z).wait_recv()
            self.colsum[z] = self.part[self.lo : self.hi, self.lanes(at.k, z)] + self.other[z]

            @pl.when(at.segment != at.q)
            def _():
                self.home(o, z, at.q, 2 * at.segment + at.k).start()

    def totals(self):
        at = self.at
        keep = jnp.where(at.folded, 0.0, 1.0).astype(jnp.float32)
        for o, z in self.order:
            self.total[z] = self.part[self.lo : self.hi, self.lanes(2, z)] * keep

            @pl.when(at.segment == at.q)
            def _():
                self.total[z] += self.colsum[z]

            @pl.when(at.mirror_folded)
            def _():
                self.mirror(o, z).wait_recv()
                self.total[z] += self.rows[z]

            for t in range(at.chips):
                @pl.when(jnp.logical_and(at.q != t, at.segment_of(t) == at.q))
                def _():
                    self.home(o, z, t, at.partner).wait_recv()
                    self.total[z] += self.cols[t, z]

            if o:
                self.move(o, z).start()

    def result(self):
        value = self.total[self.at.d]
        for o, z in self.order[:-1]:
            self.move(o, z).wait_recv()
            value = value + self.slots[o - 1]
        return value

    def close(self):
        at = self.at
        for o, z in self.order:
            if o:
                self.move(o, z).wait_send()
            self.pair(o, z).wait_send()

            @pl.when(at.folded)
            def _():
                self.mirror(o, z).wait_send()

            @pl.when(at.segment != at.q)
            def _():
                self.home(o, z, at.q, 2 * at.segment + at.k).wait_send()


def along_diag(at, slots, send, recv):
    moves = []
    for o in range(1, at.diag_size):
        peer = (at.d + o) % at.diag_size
        source = (at.d + at.diag_size - o) % at.diag_size
        out = at.copy(slots.at[at.d], slots.at[at.d], send.at[o - 1], recv.at[o - 1], peer, at.c)
        out.start()
        into = at.copy(
            slots.at[source], slots.at[source], send.at[o - 1], recv.at[o - 1], peer, at.c
        )
        moves.append((out, into))
    return moves


def along_long(at, slots, send, recv):
    moves = []
    for o in range(1, at.long_size):
        peer = (at.c + o) % at.long_size
        source = (at.c + at.long_size - o) % at.long_size
        out = at.copy(slots.at[at.c], slots.at[at.c], send.at[o - 1], recv.at[o - 1], at.d, peer)
        out.start()
        into = at.copy(
            slots.at[source], slots.at[source], send.at[o - 1], recv.at[o - 1], at.d, peer
        )
        moves.append((out, into))
    return moves


def finish(moves):
    for _, into in moves:
        into.wait_recv()
    for out, _ in moves:
        out.wait_send()


def sum_all(at, value, by_diag, by_long, sems):
    by_diag[at.d] = value
    finish(along_diag(at, by_diag, sems[0], sems[1]))
    value = by_diag[0]
    for z in range(1, at.diag_size):
        value = value + by_diag[z]
    by_long[at.c] = value
    finish(along_long(at, by_long, sems[2], sems[3]))
    value = by_long[0]
    for z in range(1, at.long_size):
        value = value + by_long[z]
    return value


def gather_kernel(sizes, x_ref, p_ref, out_ref, own, vec, send, recv):
    at = Place(*sizes)
    at.enter()
    count, states = x_ref.shape
    own[:count] = x_ref[...]
    own[count:] = p_ref[...]
    spread_panels(at, own, vec, send, recv)
    for i in range(3):
        out_ref[:, i * states : (i + 1) * states] = vec[i]


def search_kernel(sizes, part, x_ref, slice_ref, search_ref, out_ref, *scratch):
    bufs_x, bufs_p = scratch[:6], scratch[6:12]
    by_diag, by_long, pieces, own, vec = scratch[12:17]
    send_x, recv_x, send_p, recv_p = scratch[17:21]
    sums_sems, s_send, s_recv, g_send, g_recv = scratch[21:25], *scratch[25:29]
    at = Place(*sizes)
    at.enter()
    count, states = x_ref.shape
    sum_x = PanelSum(at, part, 0, count, bufs_x, send_x, recv_x)
    sum_p = PanelSum(at, part, count, 2 * count, bufs_p, send_p, recv_p)
    sum_x.start()
    sum_x.columns()
    sum_p.start()
    sum_x.totals()
    sum_p.columns()
    image = sum_x.result()
    slice_ref[:count] = image
    width = image.shape[1]
    block = x_ref[:, pl.ds(pl.multiple_of(at.d * width, 128), width)].astype(jnp.float32)
    both = jnp.concatenate([block * image, block * block], 0)
    folded = both[:, :128]
    for i in range(1, width // 128):
        folded = folded + both[:, i * 128 : (i + 1) * 128]
    sums = sum_all(at, folded, by_diag, by_long, sums_sems)
    sums = jnp.sum(sums, axis=1, keepdims=True)
    quotient = sums[:count] / sums[count:]
    pieces[at.d] = (image - quotient * block).astype(jnp.bfloat16)
    moves = along_diag(at, pieces, s_send, s_recv)
    sum_p.totals()
    finish(moves)
    for z in range(at.diag_size):
        own[:, z * width : (z + 1) * width] = pieces[z]
    spread_panels(at, own, vec, g_send, g_recv)
    search_ref[...] = own[...]
    for i in range(3):
        out_ref[:, i * states : (i + 1) * states] = vec[i]
    slice_ref[count:] = sum_p.result()
    sum_x.close()
    sum_p.close()


def project_kernel(
    sizes, part, first_ref, x_ref, search_ref, p_ref, sums_ref, image_ref,
    other, colsum, cols, rows, total, slots, by_diag, by_long, pieces, firsts, both,
    sum_send, sum_recv, z_send, z_recv, l_send, l_recv, s_send, s_recv, f_send, f_recv,
):
    at = Place(*sizes)
    at.enter()
    bufs = (other, colsum, cols, rows, total, slots)
    count = x_ref.shape[0]
    sum_w = PanelSum(at, part, 0, count, bufs, sum_send, sum_recv)
    sum_w.start()
    firsts[at.d] = first_ref[...]
    first_moves = along_diag(at, firsts, f_send, f_recv)
    sum_w.columns()
    sum_w.totals()
    image = sum_w.result()
    width = image.shape[1]
    pieces[at.d] = image
    moves = along_diag(at, pieces, s_send, s_recv)
    lanes = pl.ds(pl.multiple_of(at.d * width, 128), width)
    both[:count] = x_ref[:, lanes].astype(jnp.float32)
    both[count : 2 * count] = search_ref[:, lanes].astype(jnp.float32)
    both[2 * count : 3 * count] = p_ref[:, lanes].astype(jnp.float32)
    both[3 * count : 4 * count] = first_ref[:count]
    both[4 * count : 5 * count] = image
    both[5 * count : 6 * count] = first_ref[count:]
    both[6 * count :] = jnp.zeros((both.shape[0] - 6 * count, width), jnp.float32)
    value = lax.dot_general(
        both[: 3 * count], both[...], (((1,), (1,)), ((), ())),
        precision=HIGHEST, preferred_element_type=jnp.float32,
    )
    sums_ref[...] = sum_all(at, value, by_diag, by_long, (z_send, z_recv, l_send, l_recv))
    finish(moves)
    finish(first_moves)
    for z in range(at.diag_size):
        lanes = slice(z * width, (z + 1) * width)
        image_ref[:count, lanes] = firsts[z, :count]
        image_ref[count : 2 * count, lanes] = pieces[z]
        image_ref[2 * count :, lanes] = firsts[z, count:]
    sum_w.close()


def sum_scratch(count, states, diag_size, long_size):
    width = states // diag_size
    panel = (diag_size, count, width)
    f32 = jnp.float32
    return [
        pltpu.VMEM(panel, f32),
        pltpu.VMEM(panel, f32),
        pltpu.VMEM((long_size // 2, *panel), f32),
        pltpu.VMEM(panel, f32),
        pltpu.VMEM(panel, f32),
        pltpu.VMEM((diag_size - 1, count, width), f32),
    ]


def remote_call(kernel, sizes, collective, outs, scratch, *args):
    vmem = pl.BlockSpec(memory_space=pltpu.VMEM)
    return pl.pallas_call(
        functools.partial(kernel, sizes),
        in_specs=[vmem] * len(args),
        out_specs=[vmem] * len(outs),
        out_shape=[jax.ShapeDtypeStruct(*o) for o in outs],
        scratch_shapes=scratch,
        compiler_params=pltpu.CompilerParams(
            collective_id=collective, has_side_effects=True, vmem_limit_bytes=40 << 20
        ),
    )(*args)


def local(tiles, tile_rows, tile_cols, tile_counts, block_x, block_p):
    tile_block = tiles[0, 0]
    rows = tile_rows[0, 0]
    cols = tile_cols[0, 0]
    edge = tile_block.shape[-1]
    count, states = block_x.shape
    panel_tiles = states // edge
    diag_index = lax.axis_index("diag")
    long_index = lax.axis_index("long")
    long_size = lax.axis_size("long")
    diag_size = lax.axis_size("diag")
    folded = long_index < 2 * diag_index
    row_panel = jnp.where(folded, long_size - 1 - long_index, long_index)
    segment_id = jnp.where(folded, diag_size - 1 - diag_index, diag_index)
    meta = jnp.stack(
        [tile_counts[0, 0], row_panel * panel_tiles, 2 * segment_id * panel_tiles]
    ).astype(jnp.int32)
    sizes = (diag_size, long_size)
    width = states // diag_size
    chips = long_size // 2
    f32, bf16, dma = jnp.float32, jnp.bfloat16, pltpu.SemaphoreType.DMA
    spread_sems = [dma((chips + 2,)), dma((3,))]
    sum_sems = [dma((4 * diag_size - 1,)), dma(((3 + chips) * diag_size - 1,))]
    all_sems = [dma((n - 1,)) for n in (diag_size, diag_size, long_size, long_size)]
    diag_sems = [dma((diag_size - 1,))] * 2

    vectors = remote_call(
        gather_kernel, sizes, 1, [((2 * count, 3 * states), bf16)],
        [pltpu.VMEM((2 * count, states), bf16), pltpu.VMEM((3, 2 * count, states), bf16)]
        + spread_sems,
        block_x, block_p,
    )[0]
    part = apply_tiles(tile_block, rows, cols, meta, vectors)
    first, search, vectors = remote_call(
        search_kernel, sizes, 2,
        [((2 * count, width), f32), ((count, states), bf16), ((count, 3 * states), bf16)],
        sum_scratch(count, states, *sizes) * 2
        + [
            pltpu.VMEM((diag_size, 2 * count, 128), f32),
            pltpu.VMEM((long_size, 2 * count, 128), f32),
            pltpu.VMEM((diag_size, count, width), bf16),
            pltpu.VMEM((count, states), bf16),
            pltpu.VMEM((3, count, states), bf16),
        ]
        + sum_sems * 2 + all_sems + diag_sems + spread_sems,
        part, block_x,
    )
    part = apply_tiles(tile_block, rows, cols, meta, vectors)
    sums, himage = remote_call(
        project_kernel, sizes, 3,
        [((3 * count, 128), f32), ((3 * count, states), f32)],
        sum_scratch(count, states, *sizes)
        + [
            pltpu.VMEM((diag_size, 3 * count, 128), f32),
            pltpu.VMEM((long_size, 3 * count, 128), f32),
            pltpu.VMEM((diag_size, count, width), f32),
            pltpu.VMEM((diag_size, 2 * count, width), f32),
            pltpu.VMEM((128, width), f32),
        ]
        + sum_sems + all_sems + diag_sems * 2,
        part, first, block_x, search, block_p,
    )
    basis_in = jnp.concatenate([block_x, search, block_p], 0)
    return tuple(ritz(sums, basis_in, himage))


def solution(mesh):
    return jax.shard_map(
        local,
        mesh=mesh,
        in_specs=(
            P("diag", "long", None, None, None),
            P("diag", "long", None),
            P("diag", "long", None),
            P("diag", "long"),
            P(None, "long"),
            P(None, "long"),
        ),
        out_specs=(P(None, "long"), P(None, "long"), P()),
        check_vma=False,
    )
```

```python
import functools

import jax
import jax.numpy as jnp
from jax import lax
from jax.experimental import pallas as pl
from jax.experimental.pallas import tpu as pltpu
from jax.sharding import PartitionSpec as P

HIGHEST = lax.Precision.HIGHEST
STEP = 64
UNROLL = 64


def tile_kernel(rows_ref, cols_ref, meta_ref, vec_ref, tile_ref, out_ref):
    edge = tile_ref.shape[-1]
    row_lane = out_ref.shape[1] // 3 * 2
    base = pl.program_id(0) * STEP

    @pl.when(pl.program_id(0) == 0)
    def _():
        out_ref[...] = jnp.zeros_like(out_ref)

    count, row_off, col_off = meta_ref[0], meta_ref[1], meta_ref[2]
    live = jnp.clip(count - base, 0, STEP)

    count_vec = vec_ref.shape[0]
    blank = jnp.zeros((count_vec, edge), vec_ref.dtype)

    def spot(k):
        row = rows_ref[base + k]
        col = cols_ref[base + k]
        weight = jnp.where(row + row_off == col + col_off, 0.5, 1.0).astype(jnp.float32)
        weight = jnp.where(base + k < count, weight, 0.0)
        row_at = pl.ds(pl.multiple_of(row * edge + row_lane, edge), edge)
        col_at = pl.ds(pl.multiple_of(col * edge, edge), edge)
        return row_at, col_at, weight

    def group(i, carry):
        found = []
        for u in range(0, UNROLL, 2):
            k = i * UNROLL + u
            row_a, col_a, weight_a = spot(k)
            row_b, col_b, weight_b = spot(k + 1)
            two = tile_ref[pl.ds(k, 2)].reshape(2 * edge, edge)
            forward = lax.dot_general(
                jnp.concatenate([vec_ref[:, col_a], vec_ref[:, col_b]], 0),
                two,
                (((1,), (1,)), ((), ())),
                preferred_element_type=jnp.float32,
            )
            upper = jnp.concatenate([vec_ref[:, row_a], blank], 1)
            lower = jnp.concatenate([blank, vec_ref[:, row_b]], 1)
            backward = jnp.dot(
                jnp.concatenate([upper, lower], 0), two, preferred_element_type=jnp.float32
            )
            found.append(
                (row_a, col_a, forward[:count_vec, :edge] * weight_a, backward[:count_vec] * weight_a)
            )
            found.append(
                (row_b, col_b, forward[count_vec:, edge:] * weight_b, backward[count_vec:] * weight_b)
            )
        for row_at, col_at, forward, backward in found:
            out_ref[:, row_at] += forward
            out_ref[:, col_at] += backward
        return carry

    lax.fori_loop(0, (live + UNROLL - 1) // UNROLL, group, 0)


def apply_tiles(tiles, rows, cols, meta, vectors):
    slots, edge = tiles.shape[0], tiles.shape[-1]
    width, states = vectors.shape
    smem = pl.BlockSpec(memory_space=pltpu.SMEM)
    return pl.pallas_call(
        tile_kernel,
        grid=(slots // STEP,),
        in_specs=[
            smem,
            smem,
            smem,
            pl.BlockSpec(memory_space=pltpu.VMEM),
            pl.BlockSpec((STEP, edge, edge), lambda i: (i, 0, 0)),
        ],
        out_specs=pl.BlockSpec((width, states), lambda i: (0, 0)),
        out_shape=jax.ShapeDtypeStruct((width, states), jnp.float32),
        compiler_params=pltpu.CompilerParams(vmem_limit_bytes=40 << 20),
        cost_estimate=pl.CostEstimate(
            flops=4 * slots * edge * edge * width,
            bytes_accessed=2 * slots * edge * edge,
            transcendentals=0,
        ),
    )(rows, cols, meta, vectors, tiles)


def ritz_kernel(sums_ref, basis_ref, image_ref, rb_ref, ri_ref, rm_ref):
    size = sums_ref.shape[0]
    lane = lax.broadcasted_iota(jnp.int32, (size, size), 1)
    row = lax.broadcasted_iota(jnp.int32, (size, size), 0)
    below = lax.broadcasted_iota(jnp.int32, (size, 1), 0)
    sums = sums_ref[...]
    left = sums[:, :size]
    right = jnp.where(lane == row, 1.0, 0.0).astype(jnp.float32)
    pivots = jnp.zeros((size, 1), jnp.float32)
    for k in range(size):
        pivot = left[k : k + 1, k : k + 1]
        pivots = jnp.where(below == k, pivot, pivots)
        scale = jnp.where(below > k, left[:, k : k + 1] * (1.0 / pivot), 0.0)
        left_row, right_row = left[k : k + 1, :], right[k : k + 1, :]
        left = left - scale * left_row
        right = right - scale * right_row
    inverse = right * (1.0 / jnp.sqrt(pivots))
    nt = (((1,), (1,)), ((), ()))
    half = jnp.dot(inverse, sums[:, size : 2 * size], precision=HIGHEST, preferred_element_type=jnp.float32)
    one = lax.dot_general(half, inverse, nt, precision=HIGHEST, preferred_element_type=jnp.float32)
    two = lax.dot_general(inverse, half, nt, precision=HIGHEST, preferred_element_type=jnp.float32)
    rm_ref[...] = 0.5 * (one + two)
    rb_ref[...] = jnp.dot(
        inverse, basis_ref[...].astype(jnp.float32), precision=HIGHEST, preferred_element_type=jnp.float32
    )
    ri_ref[...] = jnp.dot(
        inverse, image_ref[...], precision=HIGHEST, preferred_element_type=jnp.float32
    )


def ritz(sums, basis, image):
    vmem = pl.BlockSpec(memory_space=pltpu.VMEM)
    like = jax.ShapeDtypeStruct(image.shape, jnp.float32)
    return pl.pallas_call(
        ritz_kernel,
        in_specs=[vmem] * 3,
        out_specs=[vmem] * 3,
        out_shape=[like, like, jax.ShapeDtypeStruct((sums.shape[0], sums.shape[0]), jnp.float32)],
        compiler_params=pltpu.CompilerParams(vmem_limit_bytes=40 << 20),
    )(sums, basis, image)


class Place:
    def __init__(self, diag_size, long_size):
        self.diag_size, self.long_size = diag_size, long_size
        self.chips = long_size // 2
        self.d = lax.axis_index("diag")
        self.c = lax.axis_index("long")
        self.q, self.k = self.c // 2, self.c % 2
        self.partner = self.q * 2 + 1 - self.k
        self.mirror = long_size - 1 - self.c
        self.folded = self.q < self.d
        self.segment = self.segment_of(self.q)
        self.mirror_folded = self.mirror // 2 < self.d

    def segment_of(self, chip):
        return jnp.where(chip < self.d, self.diag_size - 1 - self.d, self.d)

    def copy(self, src, dst, send, recv, d, c):
        return pltpu.make_async_remote_copy(
            src_ref=src,
            dst_ref=dst,
            send_sem=send,
            recv_sem=recv,
            device_id=(d, c),
            device_id_type=pl.DeviceIdType.MESH,
        )

    def enter(self):
        barrier = pltpu.get_barrier_semaphore()
        peers = [(self.d, (self.c + o) % self.long_size) for o in range(1, self.long_size)]
        peers += [((self.d + o) % self.diag_size, self.c) for o in range(1, self.diag_size)]
        for peer in peers:
            pl.semaphore_signal(barrier, inc=1, device_id=peer, device_id_type=pl.DeviceIdType.MESH)
        pl.semaphore_wait(barrier, len(peers))


def spread_panels(at, own, vec, send, recv):
    def to_chip(t):
        return at.copy(own, vec.at[at.k], send.at[t], recv.at[0], at.d, 2 * t + at.k)

    def wanted(t):
        return jnp.logical_and(at.q != t, at.segment_of(t) == at.q)

    mirror = at.copy(own, vec.at[2], send.at[at.chips], recv.at[1], at.d, at.mirror)
    for t in range(at.chips):
        @pl.when(wanted(t))
        def _():
            to_chip(t).start()

    @pl.when(at.mirror_folded)
    def _():
        mirror.start()

    pair = at.copy(
        vec.at[at.k], vec.at[at.k], send.at[at.chips + 1], recv.at[2], at.d, at.partner
    )

    @pl.when(at.segment == at.q)
    def _():
        vec[at.k] = own[...]

    @pl.when(at.segment != at.q)
    def _():
        at.copy(own, vec.at[at.k], send.at[0], recv.at[0], at.d, at.partner).wait_recv()

    pair.start()

    @pl.when(at.folded)
    def _():
        mirror.wait_recv()

    @pl.when(jnp.logical_not(at.folded))
    def _():
        vec[2] = own[...]

    pair.wait()
    for t in range(at.chips):
        @pl.when(wanted(t))
        def _():
            to_chip(t).wait_send()

    @pl.when(at.mirror_folded)
    def _():
        mirror.wait_send()


class PanelSum:
    def __init__(self, at, part, lo, hi, bufs, send, recv):
        self.at, self.part, self.lo, self.hi = at, part, lo, hi
        self.other, self.colsum, self.cols, self.rows, self.total, self.slots = bufs
        self.send, self.recv = send, recv
        size = at.diag_size
        self.width = self.total.shape[2]
        self.states = self.width * size
        self.order = [(o, (at.d + o) % size) for o in [*range(1, size), 0]]

    def lanes(self, panel, z):
        start = pl.multiple_of(panel * self.states + z * self.width, 128)
        return pl.ds(start, self.width)

    def pair(self, o, z):
        at = self.at
        return at.copy(
            self.part.at[self.lo : self.hi, self.lanes(1 - at.k, z)], self.other.at[z],
            self.send.at[o], self.recv.at[o], at.d, at.partner,
        )

    def mirror(self, o, z):
        at, size = self.at, self.at.diag_size
        return at.copy(
            self.part.at[self.lo : self.hi, self.lanes(2, z)], self.rows.at[z],
            self.send.at[size + o], self.recv.at[size + o], at.d, at.mirror,
        )

    def home(self, o, z, slot, chip):
        at, size = self.at, self.at.diag_size
        return at.copy(
            self.colsum.at[z], self.cols.at[slot, z],
            self.send.at[2 * size + o], self.recv.at[(2 + slot) * size + o],
            at.d, chip,
        )

    def move(self, o, z):
        at, size = self.at, self.at.diag_size
        return at.copy(
            self.total.at[z], self.slots.at[o - 1],
            self.send.at[3 * size + o - 1], self.recv.at[(2 + at.chips) * size + o - 1], z, at.c,
        )

    def start(self):
        for o, z in self.order:
            self.pair(o, z).start()

            @pl.when(self.at.folded)
            def _():
                self.mirror(o, z).start()

    def columns(self):
        at = self.at
        for o, z in self.order:
            self.pair(o, z).wait_recv()
            self.colsum[z] = self.part[self.lo : self.hi, self.lanes(at.k, z)] + self.other[z]

            @pl.when(at.segment != at.q)
            def _():
                self.home(o, z, at.q, 2 * at.segment + at.k).start()

    def totals(self):
        at = self.at
        keep = jnp.where(at.folded, 0.0, 1.0).astype(jnp.float32)
        for o, z in self.order:
            self.total[z] = self.part[self.lo : self.hi, self.lanes(2, z)] * keep

            @pl.when(at.segment == at.q)
            def _():
                self.total[z] += self.colsum[z]

            @pl.when(at.mirror_folded)
            def _():
                self.mirror(o, z).wait_recv()
                self.total[z] += self.rows[z]

            for t in range(at.chips):
                @pl.when(jnp.logical_and(at.q != t, at.segment_of(t) == at.q))
                def _():
                    self.home(o, z, t, at.partner).wait_recv()
                    self.total[z] += self.cols[t, z]

            if o:
                self.move(o, z).start()

    def result(self):
        value = self.total[self.at.d]
        for o, z in self.order[:-1]:
            self.move(o, z).wait_recv()
            value = value + self.slots[o - 1]
        return value

    def close(self):
        at = self.at
        for o, z in self.order:
            if o:
                self.move(o, z).wait_send()
            self.pair(o, z).wait_send()

            @pl.when(at.folded)
            def _():
                self.mirror(o, z).wait_send()

            @pl.when(at.segment != at.q)
            def _():
                self.home(o, z, at.q, 2 * at.segment + at.k).wait_send()


def along_diag(at, slots, send, recv):
    moves = []
    for o in range(1, at.diag_size):
        peer = (at.d + o) % at.diag_size
        source = (at.d + at.diag_size - o) % at.diag_size
        out = at.copy(slots.at[at.d], slots.at[at.d], send.at[o - 1], recv.at[o - 1], peer, at.c)
        out.start()
        into = at.copy(
            slots.at[source], slots.at[source], send.at[o - 1], recv.at[o - 1], peer, at.c
        )
        moves.append((out, into))
    return moves


def along_long(at, slots, send, recv):
    moves = []
    for o in range(1, at.long_size):
        peer = (at.c + o) % at.long_size
        source = (at.c + at.long_size - o) % at.long_size
        out = at.copy(slots.at[at.c], slots.at[at.c], send.at[o - 1], recv.at[o - 1], at.d, peer)
        out.start()
        into = at.copy(
            slots.at[source], slots.at[source], send.at[o - 1], recv.at[o - 1], at.d, peer
        )
        moves.append((out, into))
    return moves


def finish(moves):
    for _, into in moves:
        into.wait_recv()
    for out, _ in moves:
        out.wait_send()


def sum_all(at, value, by_diag, by_long, sems):
    by_diag[at.d] = value
    finish(along_diag(at, by_diag, sems[0], sems[1]))
    value = by_diag[0]
    for z in range(1, at.diag_size):
        value = value + by_diag[z]
    by_long[at.c] = value
    finish(along_long(at, by_long, sems[2], sems[3]))
    value = by_long[0]
    for z in range(1, at.long_size):
        value = value + by_long[z]
    return value


def gather_kernel(sizes, x_ref, p_ref, out_ref, own, vec, send, recv):
    at = Place(*sizes)
    at.enter()
    count, states = x_ref.shape
    own[:count] = x_ref[...]
    own[count:] = p_ref[...]
    spread_panels(at, own, vec, send, recv)
    for i in range(3):
        out_ref[:, i * states : (i + 1) * states] = vec[i]


def search_kernel(sizes, part, x_ref, slice_ref, search_ref, out_ref, *scratch):
    bufs_x, bufs_p = scratch[:6], scratch[6:12]
    by_diag, by_long, pieces, own, vec = scratch[12:17]
    send_x, recv_x, send_p, recv_p = scratch[17:21]
    sums_sems, s_send, s_recv, g_send, g_recv = scratch[21:25], *scratch[25:29]
    at = Place(*sizes)
    at.enter()
    count, states = x_ref.shape
    sum_x = PanelSum(at, part, 0, count, bufs_x, send_x, recv_x)
    sum_p = PanelSum(at, part, count, 2 * count, bufs_p, send_p, recv_p)
    sum_x.start()
    sum_x.columns()
    sum_p.start()
    sum_x.totals()
    sum_p.columns()
    image = sum_x.result()
    slice_ref[:count] = image
    width = image.shape[1]
    block = x_ref[:, pl.ds(pl.multiple_of(at.d * width, 128), width)].astype(jnp.float32)
    both = jnp.concatenate([block * image, block * block], 0)
    folded = both[:, :128]
    for i in range(1, width // 128):
        folded = folded + both[:, i * 128 : (i + 1) * 128]
    sums = sum_all(at, folded, by_diag, by_long, sums_sems)
    sums = jnp.sum(sums, axis=1, keepdims=True)
    quotient = sums[:count] / sums[count:]
    pieces[at.d] = (image - quotient * block).astype(jnp.bfloat16)
    moves = along_diag(at, pieces, s_send, s_recv)
    sum_p.totals()
    finish(moves)
    for z in range(at.diag_size):
        own[:, z * width : (z + 1) * width] = pieces[z]
    spread_panels(at, own, vec, g_send, g_recv)
    search_ref[...] = own[...]
    for i in range(3):
        out_ref[:, i * states : (i + 1) * states] = vec[i]
    slice_ref[count:] = sum_p.result()
    sum_x.close()
    sum_p.close()


def project_kernel(
    sizes, part, first_ref, x_ref, search_ref, p_ref, sums_ref, image_ref,
    other, colsum, cols, rows, total, slots, by_diag, by_long, pieces, firsts, both,
    sum_send, sum_recv, z_send, z_recv, l_send, l_recv, s_send, s_recv, f_send, f_recv,
):
    at = Place(*sizes)
    at.enter()
    bufs = (other, colsum, cols, rows, total, slots)
    count = x_ref.shape[0]
    sum_w = PanelSum(at, part, 0, count, bufs, sum_send, sum_recv)
    sum_w.start()
    firsts[at.d] = first_ref[...]
    first_moves = along_diag(at, firsts, f_send, f_recv)
    sum_w.columns()
    sum_w.totals()
    image = sum_w.result()
    width = image.shape[1]
    pieces[at.d] = image
    moves = along_diag(at, pieces, s_send, s_recv)
    lanes = pl.ds(pl.multiple_of(at.d * width, 128), width)
    both[:count] = x_ref[:, lanes].astype(jnp.float32)
    both[count : 2 * count] = search_ref[:, lanes].astype(jnp.float32)
    both[2 * count : 3 * count] = p_ref[:, lanes].astype(jnp.float32)
    both[3 * count : 4 * count] = first_ref[:count]
    both[4 * count : 5 * count] = image
    both[5 * count : 6 * count] = first_ref[count:]
    both[6 * count :] = jnp.zeros((both.shape[0] - 6 * count, width), jnp.float32)
    value = lax.dot_general(
        both[: 3 * count], both[...], (((1,), (1,)), ((), ())),
        precision=HIGHEST, preferred_element_type=jnp.float32,
    )
    sums_ref[...] = sum_all(at, value, by_diag, by_long, (z_send, z_recv, l_send, l_recv))
    finish(moves)
    finish(first_moves)
    for z in range(at.diag_size):
        lanes = slice(z * width, (z + 1) * width)
        image_ref[:count, lanes] = firsts[z, :count]
        image_ref[count : 2 * count, lanes] = pieces[z]
        image_ref[2 * count :, lanes] = firsts[z, count:]
    sum_w.close()


def sum_scratch(count, states, diag_size, long_size):
    width = states // diag_size
    panel = (diag_size, count, width)
    f32 = jnp.float32
    return [
        pltpu.VMEM(panel, f32),
        pltpu.VMEM(panel, f32),
        pltpu.VMEM((long_size // 2, *panel), f32),
        pltpu.VMEM(panel, f32),
        pltpu.VMEM(panel, f32),
        pltpu.VMEM((diag_size - 1, count, width), f32),
    ]


def remote_call(kernel, sizes, collective, outs, scratch, *args):
    vmem = pl.BlockSpec(memory_space=pltpu.VMEM)
    return pl.pallas_call(
        functools.partial(kernel, sizes),
        in_specs=[vmem] * len(args),
        out_specs=[vmem] * len(outs),
        out_shape=[jax.ShapeDtypeStruct(*o) for o in outs],
        scratch_shapes=scratch,
        compiler_params=pltpu.CompilerParams(
            collective_id=collective, has_side_effects=True, vmem_limit_bytes=40 << 20
        ),
    )(*args)


def local(tiles, tile_rows, tile_cols, tile_counts, block_x, block_p):
    tile_block = tiles[0, 0]
    rows = tile_rows[0, 0]
    cols = tile_cols[0, 0]
    edge = tile_block.shape[-1]
    count, states = block_x.shape
    panel_tiles = states // edge
    diag_index = lax.axis_index("diag")
    long_index = lax.axis_index("long")
    long_size = lax.axis_size("long")
    diag_size = lax.axis_size("diag")
    folded = long_index < 2 * diag_index
    row_panel = jnp.where(folded, long_size - 1 - long_index, long_index)
    segment_id = jnp.where(folded, diag_size - 1 - diag_index, diag_index)
    meta = jnp.stack(
        [tile_counts[0, 0], row_panel * panel_tiles, 2 * segment_id * panel_tiles]
    ).astype(jnp.int32)
    sizes = (diag_size, long_size)
    width = states // diag_size
    chips = long_size // 2
    f32, bf16, dma = jnp.float32, jnp.bfloat16, pltpu.SemaphoreType.DMA
    spread_sems = [dma((chips + 2,)), dma((3,))]
    sum_sems = [dma((4 * diag_size - 1,)), dma(((3 + chips) * diag_size - 1,))]
    all_sems = [dma((n - 1,)) for n in (diag_size, diag_size, long_size, long_size)]
    diag_sems = [dma((diag_size - 1,))] * 2

    vectors = remote_call(
        gather_kernel, sizes, 1, [((2 * count, 3 * states), bf16)],
        [pltpu.VMEM((2 * count, states), bf16), pltpu.VMEM((3, 2 * count, states), bf16)]
        + spread_sems,
        block_x, block_p,
    )[0]
    part = apply_tiles(tile_block, rows, cols, meta, vectors)
    first, search, vectors = remote_call(
        search_kernel, sizes, 2,
        [((2 * count, width), f32), ((count, states), bf16), ((count, 3 * states), bf16)],
        sum_scratch(count, states, *sizes) * 2
        + [
            pltpu.VMEM((diag_size, 2 * count, 128), f32),
            pltpu.VMEM((long_size, 2 * count, 128), f32),
            pltpu.VMEM((diag_size, count, width), bf16),
            pltpu.VMEM((count, states), bf16),
            pltpu.VMEM((3, count, states), bf16),
        ]
        + sum_sems * 2 + all_sems + diag_sems + spread_sems,
        part, block_x,
    )
    part = apply_tiles(tile_block, rows, cols, meta, vectors)
    sums, himage = remote_call(
        project_kernel, sizes, 3,
        [((3 * count, 128), f32), ((3 * count, states), f32)],
        sum_scratch(count, states, *sizes)
        + [
            pltpu.VMEM((diag_size, 3 * count, 128), f32),
            pltpu.VMEM((long_size, 3 * count, 128), f32),
            pltpu.VMEM((diag_size, count, width), f32),
            pltpu.VMEM((diag_size, 2 * count, width), f32),
            pltpu.VMEM((128, width), f32),
        ]
        + sum_sems + all_sems + diag_sems * 2,
        part, first, block_x, search, block_p,
    )
    basis_in = jnp.concatenate([block_x, search, block_p], 0)
    return tuple(ritz(sums, basis_in, himage))


def solution(mesh):
    return jax.shard_map(
        local,
        mesh=mesh,
        in_specs=(
            P("diag", "long", None, None, None),
            P("diag", "long", None),
            P("diag", "long", None),
            P("diag", "long"),
            P(None, "long"),
            P(None, "long"),
        ),
        out_specs=(P(None, "long"), P(None, "long"), P()),
        check_vma=False,
    )
```
